32 devices in a mesh: ctx: 2 (over y), tp: 16 (over z, x, core).
Axes of the slice: x: 2, y: 2, z: 4, core: 2. Of those that a mesh axis runs over, the one named last changes fastest.
Arguments:
- streams: bfloat16 [3, 1, 768, 8192], P(None, None, 'ctx', 'tp'), may hold values from -6 to 6
- taps: float32 [3, 7, 8192], P(None, None, 'tp'), may hold values from -2.4 to 2.4
- decay: float32 [16, 8192], P(None, 'tp'), may hold values from 0.96 to 1, as said below
- residues: float32 [16, 8192], P(None, 'tp'), may hold values from -0.12 to 0.12
- init_state: float32 [1, 16, 8192], P(None, None, 'tp'), may hold values from -48 to 48
- out_weight: bfloat16 [8192, 8192], P('tp'), may hold values from -0.09375 to 0.09375
Outputs:
- mixed: bfloat16 [1, 768, 8192], P(None, 'ctx', 'tp')
The draws below stay inside these ranges and needn't reach their ends.
Inputs may be any that keep to these rules, and one draw needn't show every extreme that they name: `decay`: each pole's factor lies strictly between 0 and 1.
All inputs are finite; a program needn't handle non-finite values.
Results may differ from the reference program's by a relative error of at most 0.0049.
Values may be sent and summed in bfloat16 or wider, within the bound.
No kernel may reach another device: no remote copies, remote signals or barrier semaphores. Data moves between devices by JAX's collectives and lax.ppermute only.
A program may use at most 128 MiB of HBM per device.

```python
import jax
import jax.numpy as jnp
from jax import lax

D = 8192
POLES = 16
TAPS = 7
SEQS = 1
WINDOW = 768


def draw_decay(key, part):
    key_pick, key_slow, key_fast = jax.random.split(jax.random.fold_in(key, 11), 3)
    slow_share = 0.5
    picked = jax.random.uniform(key_pick, (POLES, D), jnp.float32) < slow_share
    slow_rate = jnp.exp(jax.random.uniform(key_slow, (POLES, D), jnp.float32, jnp.log(0.1 / WINDOW), jnp.log(2.0 / WINDOW)))
    fast_rate = jnp.exp(jax.random.uniform(key_fast, (POLES, D), jnp.float32, jnp.log(1.0 / 50.0), jnp.log(1.0 / 30.0)))
    rate = jnp.minimum(jnp.where(picked, slow_rate, fast_rate), 1.0 / 30.0)
    return jnp.exp(-rate).astype(jnp.float32)


def spiked(entries, rng, source, target, blocks, factor):
    owner, partner = [(jnp.arange(entries.shape[position]) // (entries.shape[position] // blocks)).reshape([-1 if axis == position else 1 for axis in range(entries.ndim)]) for position in (source, target)]
    chosen = jax.random.permutation(rng, blocks)[partner]
    strong = (owner == chosen) | (owner == (partner + blocks // 2) % blocks)
    return jnp.where(strong, factor * entries, entries)


def shard_levels(key, dims, cuts, smallest, top_value):
    level, own = 1.0, jax.random.fold_in(key, 6)
    for axis_at, shards_of in cuts:
        steps = jnp.exp(jax.random.uniform(jax.random.fold_in(own, axis_at), (shards_of,), jnp.float32, smallest / len(cuts), top_value / len(cuts)))
        level = level * jnp.repeat(steps, dims[axis_at] // shards_of).reshape([-1 if axis == axis_at else 1 for axis in range(len(dims))])
    return level


def gaussian(key, extent, width, reach, shards=(), kind=jnp.bfloat16):
    result = width * jax.random.normal(key, extent, jnp.float32)
    if shards:
        result = result * shard_levels(key, extent, shards, -0.22, 0.18)
    return jnp.clip(result, -reach, reach).astype(kind)


def heavy_noise(key, shape, width, limit, cuts, heavy, held_as=jnp.bfloat16):
    values = width * jax.random.normal(key, shape, jnp.float32)
    if cuts:
        values = values * shard_levels(key, shape, cuts, -0.22, 0.18)
    return jnp.clip(spiked(values, jax.random.fold_in(key, 3), *heavy), -limit, limit).astype(held_as)


def setup_inputs(seed: int = 0) -> dict:
    streams_of = jax.random.split(jax.random.key(seed), 7)
    return {
        "streams": gaussian(streams_of[0], (3, SEQS, WINDOW, D), 1.0, 6.0, ((2, 2), (3, 16))),
        "taps": gaussian(streams_of[1], (3, TAPS, D), 0.4, 2.4, ((2, 16),), jnp.float32),
        "decay": draw_decay(jax.random.fold_in(streams_of[6], 71), 0),
        "residues": gaussian(streams_of[3], (POLES, D), 0.02, 0.12, ((1, 16),), jnp.float32),
        "init_state": gaussian(streams_of[4], (SEQS, POLES, D), 8.0, 48.0, ((2, 16),), jnp.float32),
        "out_weight": heavy_noise(streams_of[5], (D, D), D ** -0.5, 0.09375, ((0, 16),), (0, 1, 16, 2.0)),
    }


def reference(streams, taps, decay, residues, init_state, out_weight):
    tap_lag = TAPS - 1
    widened = jnp.pad(streams.astype(jnp.float32), ((0, 0), (0, 0), (tap_lag, 0), (0, 0)))
    featured = jnp.zeros(streams.shape, jnp.float32)
    for tap_index in range(TAPS):
        featured = featured + taps[:, tap_index][:, None, None, :] * widened[:, :, tap_lag - tap_index:tap_lag - tap_index + WINDOW, :]
    queries = featured[0]
    driven = featured[1] * featured[2]

    def advance(running, driven_now):
        running = decay[None] * running + driven_now[:, None, :]
        return running, jnp.sum(residues[None] * running, axis=1)

    _, outputs = lax.scan(advance, init_state, jnp.swapaxes(driven, 0, 1))
    response = jnp.swapaxes(outputs, 0, 1)
    gated_out = (queries * response).astype(jnp.bfloat16)
    mixed = jnp.dot(gated_out.reshape(SEQS * WINDOW, D), out_weight, preferred_element_type=jnp.float32)
    return mixed.astype(jnp.bfloat16).reshape(SEQS, WINDOW, D)
```

```python
import functools

import jax
import jax.numpy as jnp
from jax import lax
from jax.experimental import pallas as pl
from jax.experimental.pallas import tpu as pltpu
from jax.sharding import PartitionSpec as P

F32 = jnp.float32
BF16 = jnp.bfloat16
LANES = 128
SEGS = 8
PAD = 8


def power(base, exponent):
    result, square = None, base
    while exponent:
        if exponent & 1:
            result = square if result is None else result * square
        exponent >>= 1
        if exponent:
            square = square * square
    return result


def tree_sum(terms):
    while len(terms) > 1:
        paired = [a + b for a, b in zip(terms[::2], terms[1::2])]
        terms = paired + terms[len(paired) * 2 :]
    return terms[0]


def driven_kernel(where_ref, streams_ref, taps_ref, decay_ref, init_ref, weight_ref, driven_ref, inner_ref, message_ref, sent_ref, wide_ref, sems):
    first = where_ref[0] == 0
    core = where_ref[1]
    poles = decay_ref.shape[0]
    tap_count = taps_ref.shape[1]
    length, channels = streams_ref.shape[2:]
    tiles = channels // LANES
    seg_len = length // SEGS
    width = sent_ref.shape[2]
    copies = []
    for part in range(sent_ref.shape[0]):
        column = pl.multiple_of((2 * part + 1 - core) * width, LANES)
        copy = pltpu.make_async_copy(weight_ref.at[:, pl.ds(column, width)], sent_ref.at[part], sems.at[part])
        copy.start()
        copies.append(copy)
    sublane = lax.broadcasted_iota(jnp.int32, (SEGS, LANES), 0)
    early = jnp.logical_and(sublane == 0, jnp.logical_not(first))
    for tile in range(tiles):
        lanes = slice(tile * LANES, (tile + 1) * LANES)
        for s in range(2):
            wide_ref[s, 0:PAD, :] = jnp.zeros((PAD, LANES), F32)
            wide_ref[s, PAD : PAD + length, :] = streams_ref[1 + s, 0, :, lanes].astype(F32)
        taps = [[jnp.broadcast_to(taps_ref[1 + s, i : i + 1, lanes], (SEGS, LANES)) for i in range(tap_count)] for s in range(2)]

        def row(s, j):
            return wide_ref[s, pl.ds(PAD + j, SEGS, stride=seg_len), :]

        def block(base, windows, masked):
            windows = list(windows)
            for step in range(8):
                made = []
                for s in range(2):
                    seen = list(windows[s]) + [row(s, base + step)]
                    made.append(tree_sum([taps[s][i] * seen[-1 - i] for i in range(tap_count)]))
                    windows[s] = tuple(seen[1:])
                product = made[0] * made[1]
                if masked and step < tap_count - 1:
                    product = jnp.where(early, 0.0, product)
                driven_ref[tile, base + step] = product
            return tuple(windows)

        windows = tuple(tuple(row(s, j - (tap_count - 1)) for j in range(tap_count - 1)) for s in range(2))
        windows = block(0, windows, True)
        lax.fori_loop(1, seg_len // 8, lambda b, w: block(b * 8, w, False), windows)

        decays = [jnp.broadcast_to(decay_ref[n : n + 1, lanes], (SEGS, LANES)) for n in range(poles)]

        def scan(b, states):
            states = list(states)
            for step in range(8):
                value = driven_ref[tile, b * 8 + step]
                states = [d * s + value for d, s in zip(decays, states)]
            return tuple(states)

        zero = jnp.zeros((SEGS, LANES), F32)
        ends = lax.fori_loop(0, seg_len // 8, scan, (zero,) * poles)
        for n in range(poles):
            total, factor = ends[n], power(decays[n], seg_len)
            for reach in (1, 2, 4):
                moved = jnp.where(sublane >= reach, pltpu.roll(total, reach, 0), 0.0)
                total = total + factor * moved
                factor = factor * factor
            inner_ref[tile, n] = total
            message_ref[n : n + 1, lanes] = total[SEGS - 1 : SEGS, :]
    carried = power(decay_ref[...], length) * init_ref[0]
    message_ref[0:poles, :] = message_ref[0:poles, :] + jnp.where(first, carried, 0.0)
    for s in range(3):
        message_ref[poles + s * PAD : poles + (s + 1) * PAD, :] = streams_ref[s, 0, length - 16 :, :].astype(F32)[16 - PAD :]
    for copy in copies:
        copy.wait()


def gated_kernel(where_ref, message_ref, streams_ref, taps_ref, decay_ref, residues_ref, init_ref, driven_in_ref, inner_ref, gated_ref, driven_ref, wide_ref, query_ref, head_ref, start_ref, out_ref):
    first = where_ref[0] == 0
    poles = decay_ref.shape[0]
    tap_count = taps_ref.shape[1]
    lag = tap_count - 1
    length, channels = streams_ref.shape[2:]
    tiles = channels // LANES
    seg_len = length // SEGS
    sublane = lax.broadcasted_iota(jnp.int32, (SEGS, LANES), 0)

    head = []
    for s in range(2):
        head_ref[0:PAD, :] = message_ref[poles + (1 + s) * PAD : poles + (2 + s) * PAD, :]
        head_ref[PAD : PAD + 16, :] = streams_ref[1 + s, 0, 0:16, :].astype(F32)
        head.append(tree_sum([taps_ref[1 + s, i : i + 1, :] * head_ref[PAD - i : 2 * PAD - i, :] for i in range(tap_count)]))
    head = head[0] * head[1]
    decay = decay_ref[...]
    state = jnp.where(first, init_ref[0], message_ref[0:poles, :])
    start_ref[0:poles, :] = state
    counted = jnp.where(first, 0.0, head)
    for j in range(lag):
        state = decay * state + counted[j : j + 1, :]
    start_ref[poles:, :] = state * power(decay, seg_len - lag)

    for tile in range(tiles):
        lanes = slice(tile * LANES, (tile + 1) * LANES)
        driven_ref[...] = driven_in_ref[tile]
        for j in range(lag):
            driven_ref[j, 0:1, :] = head[j : j + 1, lanes]
        wide_ref[0:PAD, :] = message_ref[poles : poles + PAD, lanes]
        wide_ref[PAD : PAD + length, :] = streams_ref[0, 0, :, lanes].astype(F32)
        taps = [jnp.broadcast_to(taps_ref[0, i : i + 1, lanes], (SEGS, LANES)) for i in range(tap_count)]

        def row(j):
            return wide_ref[pl.ds(PAD + j, SEGS, stride=seg_len), :]

        def fir(b, window):
            window = list(window)
            for step in range(8):
                window.append(row(b * 8 + step))
                query_ref[b * 8 + step] = tree_sum([taps[i] * window[-1 - i] for i in range(tap_count)])
                window = window[1:]
            return tuple(window)

        lax.fori_loop(0, seg_len // 8, fir, tuple(row(j - lag) for j in range(lag)))

        decays = [jnp.broadcast_to(decay_ref[n : n + 1, lanes], (SEGS, LANES)) for n in range(poles)]
        weights = [jnp.broadcast_to(residues_ref[n : n + 1, lanes], (SEGS, LANES)) for n in range(poles)]
        states = []
        for n in range(poles):
            factor = power(decays[n], seg_len)
            spread = jnp.broadcast_to(start_ref[poles + n : poles + n + 1, lanes], (SEGS, LANES))
            before = sublane - 1
            for bit in (1, 2, 4):
                spread = jnp.where(jnp.bitwise_and(before, bit) != 0, spread * factor, spread)
                factor = factor * factor
            entry = pltpu.roll(inner_ref[tile, n], 1, 0) + spread
            own = jnp.broadcast_to(start_ref[n : n + 1, lanes], (SEGS, LANES))
            states.append(jnp.where(sublane == 0, own, entry))

        def scan(b, states):
            states = list(states)
            for step in range(8):
                value = driven_ref[b * 8 + step]
                states = [d * s + value for d, s in zip(decays, states)]
                response = tree_sum([r * s for r, s in zip(weights, states)])
                out_ref[pl.ds(b * 8 + step, SEGS, stride=seg_len), :] = response * query_ref[b * 8 + step]
            return tuple(states)

        lax.fori_loop(0, seg_len // 8, scan, tuple(states))
        gated_ref[:, lanes] = out_ref[...].astype(BF16)


def project_kernel(where_ref, own_ref, other_ref, wos_ref, wok_ref, wts_ref, wtk_ref, send_ref, keep_ref):
    cut = wos_ref.shape[1]
    mine = jnp.concatenate([wos_ref[...], wok_ref[...]], axis=1)
    theirs = jnp.concatenate([wts_ref[0], wtk_ref[0]], axis=1)
    total = jnp.dot(own_ref[...], mine, preferred_element_type=F32) + jnp.dot(other_ref[...], theirs, preferred_element_type=F32)
    send_ref[0] = total[:, :cut].astype(BF16)
    keep_ref[0] = total[:, cut:]


def project(where, own, other, weight, swapped, order, part, cut):
    length, channels = own.shape
    halves, _, width = swapped.shape
    rest = halves // 2
    cuts = width // cut

    def relative(index, high):
        value = high << (order[0] - 1)
        count = len(order) - 1
        for place, bit in enumerate(order[1:]):
            value = value | (((index >> (count - 1 - place)) & 1) << (bit - 1))
        return value

    def column(high):
        def at(index, where_ref):
            block = relative(index, high) ^ where_ref[2]
            return (0, (2 * block + where_ref[1]) * cuts + part)

        return at

    def swapped_at(high):
        return lambda index, where_ref: (relative(index, high) ^ where_ref[2], 0, part)

    whole = pl.BlockSpec((length, channels), lambda index, where_ref: (0, 0))
    flops = 2 * length * 2 * channels * halves * cut
    moved = 2 * channels * halves * cut * 2 + 6 * rest * length * cut
    return pl.pallas_call(
        project_kernel,
        out_shape=(jax.ShapeDtypeStruct((rest, length, cut), BF16), jax.ShapeDtypeStruct((rest, length, cut), F32)),
        grid_spec=pltpu.PrefetchScalarGridSpec(
            num_scalar_prefetch=1,
            grid=(rest,),
            in_specs=[
                whole,
                whole,
                pl.BlockSpec((channels, cut), column(1)),
                pl.BlockSpec((channels, cut), column(0)),
                pl.BlockSpec((1, channels, cut), swapped_at(1)),
                pl.BlockSpec((1, channels, cut), swapped_at(0)),
            ],
            out_specs=(
                pl.BlockSpec((1, length, cut), lambda index, where_ref: (index, 0, 0)),
                pl.BlockSpec((1, length, cut), lambda index, where_ref: (index, 0, 0)),
            ),
        ),
        compiler_params=pltpu.CompilerParams(vmem_limit_bytes=24 * 1024 * 1024),
        cost_estimate=pl.CostEstimate(flops=flops, bytes_accessed=moved, transcendentals=0),
        name="project",
    )(where, own, other, weight, weight, swapped, swapped)


def across(x, bit):
    count = lax.axis_size("tp")
    return lax.ppermute(x, "tp", [(i, i ^ (1 << bit)) for i in range(count)])


def after(x, axis):
    count = lax.axis_size(axis)
    return lax.ppermute(x, axis, [(i, i + 1) for i in range(count - 1)])


def later_rounds(message, inner_end, streams, taps, decay, init_state):
    first = lax.axis_index("ctx") == 0
    poles = decay.shape[0]
    tap_count = taps.shape[1]
    lag = tap_count - 1
    length = streams.shape[2]
    rims = message[poles:].reshape(3, PAD, -1)
    joined = jnp.concatenate([rims, streams[:, 0, :PAD].astype(F32)], axis=1)
    featured = sum(taps[:, i][:, None, :] * joined[:, PAD - i : 2 * PAD - i, :] for i in range(tap_count))
    head = jnp.where(first, 0.0, featured[1] * featured[2])
    local = jnp.where(first, 0.0, inner_end)

    def one(_, incoming):
        state = jnp.where(first, init_state[0], incoming)
        for j in range(lag):
            state = decay * state + head[j][None]
        ended = jnp.where(first, inner_end, local + power(decay, length - lag) * state)
        return after(ended, "ctx")

    state = lax.fori_loop(0, lax.axis_size("ctx") - 2, one, message[:poles])
    return jnp.concatenate([state, message[poles:]], axis=0)


def per_device(streams, taps, decay, residues, init_state, out_weight):
    length, channels = streams.shape[2:]
    poles = decay.shape[0]
    tiles = channels // LANES
    seg_len = length // SEGS
    peers = lax.axis_size("tp")
    width = out_weight.shape[1] // peers
    me = lax.axis_index("tp")
    where = jnp.stack([lax.axis_index("ctx"), me & 1, me >> 1]).astype(jnp.int32)
    smem = pl.BlockSpec(memory_space=pltpu.SMEM)
    vmem = pl.BlockSpec(memory_space=pltpu.VMEM)
    hbm = pl.BlockSpec(memory_space=pl.ANY)
    rows = poles + 3 * PAD
    driven, inner, message, sent = pl.pallas_call(
        driven_kernel,
        out_shape=(
            jax.ShapeDtypeStruct((tiles, seg_len, SEGS, LANES), F32),
            jax.ShapeDtypeStruct((tiles, poles, SEGS, LANES), F32),
            jax.ShapeDtypeStruct((rows, channels), F32),
            jax.ShapeDtypeStruct((peers // 2, channels, width), BF16),
        ),
        in_specs=[smem, vmem, vmem, vmem, vmem, hbm],
        out_specs=(vmem, vmem, vmem, hbm),
        scratch_shapes=[pltpu.VMEM((2, PAD + length, LANES), F32), pltpu.SemaphoreType.DMA((peers // 2,))],
        compiler_params=pltpu.CompilerParams(vmem_limit_bytes=24 * 1024 * 1024),
        cost_estimate=pl.CostEstimate(flops=10_000_000, bytes_accessed=12_000_000, transcendentals=0),
        name="driven",
    )(where, streams, taps, decay, init_state, out_weight)
    passed = after(message, "ctx")
    swapped = across(sent, 0)
    if lax.axis_size("ctx") > 2:
        passed = later_rounds(passed, message[:poles], streams, taps, decay, init_state)
    gated = pl.pallas_call(
        gated_kernel,
        out_shape=jax.ShapeDtypeStruct((length, channels), BF16),
        in_specs=[smem] + [vmem] * 8,
        out_specs=vmem,
        scratch_shapes=[
            pltpu.VMEM((seg_len, SEGS, LANES), F32),
            pltpu.VMEM((PAD + length, LANES), F32),
            pltpu.VMEM((seg_len, SEGS, LANES), F32),
            pltpu.VMEM((PAD + 16, channels), F32),
            pltpu.VMEM((2 * poles, channels), F32),
            pltpu.VMEM((length, LANES), F32),
        ],
        compiler_params=pltpu.CompilerParams(vmem_limit_bytes=24 * 1024 * 1024),
        cost_estimate=pl.CostEstimate(flops=10_000_000, bytes_accessed=3_000_000, transcendentals=0),
        name="gated",
    )(where, passed, streams, taps, decay, residues, init_state, driven, inner)
    other = across(gated, 0)

    bits = tuple(range(1, peers.bit_length() - 1))
    cut = LANES
    finished = []
    for part in range(width // cut):
        order = bits
        send, keep = project(where, gated, other, out_weight, swapped, order, part, cut)
        for place, bit in enumerate(order):
            received = across(send, bit).astype(F32)
            total = keep + received
            half = total.shape[0] // 2
            if place + 1 < len(order):
                send, keep = total[half:].astype(BF16), total[:half]
            else:
                finished.append(total[0].astype(BF16))
    return jnp.concatenate(finished, axis=-1)[None]


def solution(mesh):
    in_specs = (
        P(None, None, "ctx", "tp"),
        P(None, None, "tp"),
        P(None, "tp"),
        P(None, "tp"),
        P(None, None, "tp"),
        P("tp", None),
    )
    out_specs = P(None, "ctx", "tp")
    return jax.shard_map(
        per_device, mesh=mesh, in_specs=in_specs, out_specs=out_specs, check_vma=False
    )
```

```python
import dataclasses
import functools

import jax
import jax.numpy as jnp
from jax import lax
from jax.experimental import pallas as pl
from jax.experimental.pallas import tpu as pltpu
from jax.sharding import PartitionSpec as P

F32 = jnp.float32
BF16 = jnp.bfloat16
LANES = 128
SEGS = 8
PAD = 8
EDGE = 2 * PAD


def power(base, exponent):
    result, square = None, base
    while exponent:
        if exponent & 1:
            result = square if result is None else result * square
        exponent >>= 1
        if exponent:
            square = square * square
    return result


def segments(length):
    seg_len = (length + PAD) // SEGS
    return seg_len, next(n for n in (7, 8, 6, 5, 4, 3, 2, 1) if seg_len % n == 0)


def tree_sum(terms):
    while len(terms) > 1:
        paired = [a + b for a, b in zip(terms[::2], terms[1::2])]
        terms = paired + terms[len(paired) * 2 :]
    return terms[0]


def weight_columns(weight_hbm, ref, side, sems):
    width = ref.shape[2]
    copies = []
    for part in range(ref.shape[0]):
        column = pl.multiple_of((2 * part + side) * width, LANES)
        copies.append(pltpu.make_async_copy(weight_hbm.at[:, pl.ds(column, width)], ref.at[part], sems.at[part]))
    return copies


def driven_kernel(where_ref, streams_hbm, taps_hbm, decay_hbm, init_hbm, weight_hbm, driven_ref, inner_ref, message_ref, sent_ref, wide_ref, streams_ref, rim_ref, taps_ref, decay_ref, init_ref, weight_sems, sems):
    first = where_ref[0] == 0
    core = where_ref[1]
    poles = decay_ref.shape[0]
    tap_count = taps_ref.shape[1]
    length, channels = streams_hbm.shape[2:]
    tiles = channels // LANES
    seg_len, turn = segments(length)
    heads = -(-(PAD + tap_count) // turn)
    small = [
        pltpu.make_async_copy(taps_hbm, taps_ref, sems.at[0]),
        pltpu.make_async_copy(decay_hbm, decay_ref, sems.at[1]),
        pltpu.make_async_copy(init_hbm, init_ref, sems.at[2]),
        pltpu.make_async_copy(streams_hbm.at[:, 0, length - 16 :], rim_ref, sems.at[3]),
    ]
    loads = []
    for tile in range(tiles):
        lanes = pl.ds(tile * LANES, LANES)
        loads.append(pltpu.make_async_copy(streams_hbm.at[1:3, 0, :, lanes], streams_ref.at[tile], sems.at[4 + tile]))
    loads[0].start()
    for copy in small + loads[1:]:
        copy.start()
    copies = weight_columns(weight_hbm, sent_ref, 1 - core, weight_sems)
    for copy in copies:
        copy.start()
    for copy in small:
        copy.wait()
    sublane = lax.broadcasted_iota(jnp.int32, (SEGS, LANES), 0)
    early = jnp.logical_and(sublane == 0, jnp.logical_not(first))
    for tile in range(tiles):
        lanes = slice(tile * LANES, (tile + 1) * LANES)
        loads[tile].wait()
        for s in range(2):
            wide_ref[s, 0:EDGE, :] = jnp.zeros((EDGE, LANES), F32)
            wide_ref[s, EDGE : EDGE + length, :] = streams_ref[tile, s].astype(F32)
        taps = [[jnp.broadcast_to(taps_ref[1 + s, i : i + 1, lanes], (SEGS, LANES)) for i in range(tap_count)] for s in range(2)]

        def row(s, j):
            return wide_ref[s, pl.ds(PAD + j, SEGS, stride=seg_len), :]

        def block(base, windows, masked):
            windows = list(windows)
            for step in range(turn):
                made = []
                for s in range(2):
                    seen = list(windows[s]) + [row(s, base + step)]
                    made.append(tree_sum([taps[s][i] * seen[-1 - i] for i in range(tap_count)]))
                    windows[s] = tuple(seen[1:])
                product = made[0] * made[1]
                if masked and PAD <= base + step < PAD + tap_count - 1:
                    product = jnp.where(early, 0.0, product)
                driven_ref[tile, base + step] = product
            return tuple(windows)

        windows = tuple(tuple(row(s, j - (tap_count - 1)) for j in range(tap_count - 1)) for s in range(2))
        for b in range(heads):
            windows = block(b * turn, windows, True)
        lax.fori_loop(heads, seg_len // turn, lambda b, w: block(b * turn, w, False), windows)

        decays = [jnp.broadcast_to(decay_ref[n : n + 1, lanes], (SEGS, LANES)) for n in range(poles)]

        def scan(b, states):
            states = list(states)
            for step in range(turn):
                value = driven_ref[tile, b * turn + step]
                states = [d * s + value for d, s in zip(decays, states)]
            return tuple(states)

        zero = jnp.zeros((SEGS, LANES), F32)
        ends = lax.fori_loop(0, seg_len // turn, scan, (zero,) * poles)
        for n in range(poles):
            total, factor = ends[n], power(decays[n], seg_len)
            for reach in (1, 2, 4):
                moved = jnp.where(sublane >= reach, pltpu.roll(total, reach, 0), 0.0)
                total = total + factor * moved
                factor = factor * factor
            inner_ref[tile, n] = total
            message_ref[n : n + 1, lanes] = total[SEGS - 1 : SEGS, :]
    carried = power(decay_ref[...], length) * init_ref[0]
    message_ref[0:poles, :] = message_ref[0:poles, :] + jnp.where(first, carried, 0.0)
    for s in range(3):
        message_ref[poles + s * PAD : poles + (s + 1) * PAD, :] = rim_ref[s].astype(F32)[16 - PAD :]
    for copy in copies:
        copy.wait()


def response_kernel(where_ref, query_in_ref, taps_ref, decay_ref, residues_ref, driven_ref, inner_ref, weight_hbm, response_ref, query_ref, mine_ref, wide_ref, weight_sems):
    poles = decay_ref.shape[0]
    tap_count = taps_ref.shape[1]
    lag = tap_count - 1
    length, channels = query_in_ref.shape[2:]
    tiles = channels // LANES
    seg_len, turn = segments(length)
    copies = weight_columns(weight_hbm, mine_ref, where_ref[1], weight_sems)
    for copy in copies:
        copy.start()
    sublane = lax.broadcasted_iota(jnp.int32, (SEGS, LANES), 0)
    for tile in range(tiles):
        lanes = slice(tile * LANES, (tile + 1) * LANES)
        wide_ref[0:EDGE, :] = jnp.zeros((EDGE, LANES), F32)
        wide_ref[EDGE : EDGE + length, :] = query_in_ref[0, 0, :, lanes].astype(F32)
        taps = [jnp.broadcast_to(taps_ref[0, i : i + 1, lanes], (SEGS, LANES)) for i in range(tap_count)]

        def row(j):
            return wide_ref[pl.ds(PAD + j, SEGS, stride=seg_len), :]

        def fir(b, window):
            window = list(window)
            for step in range(turn):
                window.append(row(b * turn + step))
                query_ref[tile, b * turn + step] = tree_sum([taps[i] * window[-1 - i] for i in range(tap_count)])
                window = window[1:]
            return tuple(window)

        lax.fori_loop(0, seg_len // turn, fir, tuple(row(j - lag) for j in range(lag)))

        decays = [jnp.broadcast_to(decay_ref[n : n + 1, lanes], (SEGS, LANES)) for n in range(poles)]
        weights = [jnp.broadcast_to(residues_ref[n : n + 1, lanes], (SEGS, LANES)) for n in range(poles)]
        states = [jnp.where(sublane == 0, 0.0, pltpu.roll(inner_ref[tile, n], 1, 0)) for n in range(poles)]

        def scan(b, states):
            states = list(states)
            for step in range(turn):
                value = driven_ref[tile, b * turn + step]
                states = [d * s + value for d, s in zip(decays, states)]
                response_ref[tile, b * turn + step] = tree_sum([r * s for r, s in zip(weights, states)])
            return tuple(states)

        lax.fori_loop(0, seg_len // turn, scan, tuple(states))
    for copy in copies:
        copy.wait()


def gated_kernel(where_ref, message_ref, head_in_ref, taps_ref, decay_ref, residues_ref, init_ref, response_ref, query_ref, gated_ref, head_ref, start_ref, out_ref):
    first = where_ref[0] == 0
    poles = decay_ref.shape[0]
    tap_count = taps_ref.shape[1]
    lag = tap_count - 1
    length, channels = gated_ref.shape
    tiles = channels // LANES
    seg_len, turn = segments(length)
    heads_count = -(-(PAD + tap_count) // turn)
    sublane = lax.broadcasted_iota(jnp.int32, (SEGS, LANES), 0)

    heads = []
    for s in range(3):
        head_ref[0:PAD, :] = message_ref[poles + s * PAD : poles + (s + 1) * PAD, :]
        head_ref[PAD : PAD + 16, :] = head_in_ref[s, 0, 0:16, :].astype(F32)
        heads.append(tree_sum([taps_ref[s, i : i + 1, :] * head_ref[PAD - i : 2 * PAD - i, :] for i in range(tap_count)]))
    head_query = heads[0]
    counted = jnp.where(first, 0.0, heads[1] * heads[2])
    decay = decay_ref[...]
    state = jnp.where(first, init_ref[0], message_ref[0:poles, :])
    start_ref[0:poles, :] = state * residues_ref[...]
    for j in range(lag):
        state = decay * state + counted[j : j + 1, :]
    start_ref[poles:, :] = state * residues_ref[...] * power(decay, seg_len - PAD - lag)

    for tile in range(tiles):
        lanes = slice(tile * LANES, (tile + 1) * LANES)
        decays = [jnp.broadcast_to(decay_ref[n : n + 1, lanes], (SEGS, LANES)) for n in range(poles)]
        states = []
        for n in range(poles):
            factor = power(decays[n], seg_len)
            spread = jnp.broadcast_to(start_ref[poles + n : poles + n + 1, lanes], (SEGS, LANES))
            before = sublane - 1
            for bit in (1, 2, 4):
                spread = jnp.where(jnp.bitwise_and(before, bit) != 0, spread * factor, spread)
                factor = factor * factor
            states.append(jnp.where(sublane == 0, 0.0, spread))

        def block(b, states, head):
            states = list(states)
            for step in range(turn):
                at = b * turn + step
                query = query_ref[tile, at]
                if head and at == PAD:
                    states = [jnp.where(sublane == 0, jnp.broadcast_to(start_ref[n : n + 1, lanes], (SEGS, LANES)), s) for n, s in enumerate(states)]
                states = [d * s for d, s in zip(decays, states)]
                if head and PAD <= at < PAD + lag:
                    j = at - PAD
                    value = jnp.where(sublane == 0, jnp.broadcast_to(counted[j : j + 1, lanes], (SEGS, LANES)), 0.0)
                    states = [s + value * jnp.broadcast_to(residues_ref[n : n + 1, lanes], (SEGS, LANES)) for n, s in enumerate(states)]
                    query = jnp.where(sublane == 0, jnp.broadcast_to(head_query[j : j + 1, lanes], (SEGS, LANES)), query)
                total = response_ref[tile, at] + tree_sum(states)
                out_ref[pl.ds(at, SEGS, stride=seg_len), :] = total * query
            return tuple(states)

        for b in range(heads_count):
            states = block(b, states, True)
        lax.fori_loop(heads_count, seg_len // turn, lambda b, states: block(b, states, False), states)
        gated_ref[:, lanes] = out_ref[PAD:, :].astype(BF16)


def relative(index, high, order):
    value = high << (order[0] - 1)
    count = len(order) - 1
    for place, bit in enumerate(order[1:]):
        value = value | (((index >> (count - 1 - place)) & 1) << (bit - 1))
    return value


def project_kernel(part, where_ref, own_ref, other_ref, mine_ref, theirs_ref, order_ref, send_ref, keep_ref):
    row, rows, column, columns = part.box
    take = slice(column, column + columns)
    wide = jnp.concatenate([own_ref[row : row + rows, :], other_ref[row : row + rows, :]], axis=1)

    def step(index, carry):
        sides = []
        for high in (1, 0):
            block = relative(index, high, part.order) ^ where_ref[2]
            sides.append(jnp.concatenate([mine_ref[block, :, take], theirs_ref[block, :, take]], axis=0))
        total = jnp.dot(wide, jnp.concatenate(sides, axis=1), preferred_element_type=F32)
        send_ref[index] = total[:, :columns].astype(BF16)
        keep_ref[index] = total[:, columns:]
        return carry

    lax.fori_loop(0, send_ref.shape[0], step, 0)


def merge_kernel(keep_ref, received_ref, order_ref, send_ref, kept_ref):
    half = kept_ref.shape[0]
    send_ref[...] = (keep_ref[half:] + received_ref[half:].astype(F32)).astype(BF16)
    kept_ref[...] = keep_ref[:half] + received_ref[:half].astype(F32)


def finish_kernel(keep_ref, received_ref, order_ref, out_ref):
    out_ref[...] = (keep_ref[0] + received_ref[0].astype(F32)).astype(BF16)


def gather_kernel(boxes, *refs):
    count = len(boxes) - 1
    pieces, (keep_ref, received_ref, order_ref, out_ref, last_ref, sems) = refs[:count], refs[count:]
    copies = []
    for at, (piece, (row, rows, column, columns)) in enumerate(zip(list(pieces) + [last_ref], boxes)):
        if at == count:
            last_ref[...] = (keep_ref[0] + received_ref[0].astype(F32)).astype(BF16)
        place = out_ref.at[0, pl.ds(row, rows), pl.ds(column, columns)]
        copies.append(pltpu.make_async_copy(piece, place, sems.at[at]))
        copies[-1].start()
    for copy in copies:
        copy.wait()


SMEM = pl.BlockSpec(memory_space=pltpu.SMEM)
VMEM = pl.BlockSpec(memory_space=pltpu.VMEM)
HBM = pl.BlockSpec(memory_space=pltpu.HBM)
ANYWHERE = pl.BlockSpec(memory_space=pl.ANY)
LIMIT = 24 * 1024 * 1024
QUICK = pl.CostEstimate(flops=1, bytes_accessed=1, transcendentals=0)


def in_hbm(x):
    return pltpu.with_memory_space_constraint(x, pltpu.MemorySpace.HBM)


@dataclasses.dataclass(frozen=True)
class Part:
    box: tuple
    order: tuple


def project(part, where, own, other, mine, theirs, ordered):
    channels = own.shape[1]
    halves = mine.shape[0]
    rest = halves // 2
    _, rows, _, columns = part.box
    return pl.pallas_call(
        functools.partial(project_kernel, part),
        out_shape=(jax.ShapeDtypeStruct((rest, rows, columns), BF16), jax.ShapeDtypeStruct((rest, rows, columns), F32)),
        in_specs=[SMEM, VMEM, VMEM, VMEM, VMEM, ANYWHERE],
        out_specs=(VMEM, VMEM),
        compiler_params=pltpu.CompilerParams(vmem_limit_bytes=LIMIT),
        cost_estimate=QUICK,
        name="project",
    )(where, own, other, mine, theirs, ordered)


def merge(keep, received, ordered):
    half = keep.shape[0] // 2
    shape = (half,) + keep.shape[1:]
    return pl.pallas_call(
        merge_kernel,
        out_shape=(jax.ShapeDtypeStruct(shape, BF16), jax.ShapeDtypeStruct(shape, F32)),
        in_specs=[VMEM, VMEM, ANYWHERE],
        out_specs=(VMEM, VMEM),
        compiler_params=pltpu.CompilerParams(vmem_limit_bytes=LIMIT),
        cost_estimate=QUICK,
        name="merge",
    )(keep, received, ordered)


def finish(keep, received, ordered):
    return pl.pallas_call(
        finish_kernel,
        out_shape=jax.ShapeDtypeStruct(keep.shape[1:], BF16),
        in_specs=[VMEM, VMEM, ANYWHERE],
        out_specs=VMEM,
        compiler_params=pltpu.CompilerParams(vmem_limit_bytes=LIMIT),
        cost_estimate=QUICK,
        name="finish",
    )(keep, received, ordered)


def gather(pieces, boxes, keep, received, ordered, length, width):
    return pl.pallas_call(
        functools.partial(gather_kernel, boxes),
        out_shape=jax.ShapeDtypeStruct((1, length, width), BF16),
        in_specs=[VMEM] * len(pieces) + [VMEM, VMEM, ANYWHERE],
        out_specs=HBM,
        scratch_shapes=[pltpu.VMEM(keep.shape[1:], BF16), pltpu.SemaphoreType.DMA((len(boxes),))],
        compiler_params=pltpu.CompilerParams(vmem_limit_bytes=LIMIT),
        cost_estimate=QUICK,
        name="gather",
    )(*pieces, keep, received, ordered)


def plan(peers, length, width):
    bits = tuple(range(1, peers.bit_length() - 1))
    far = bits[-2:] + bits[:-2]
    count = width // LANES
    if count == 4 and len(bits) == 3 and length % 48 == 0:
        third = length // 3
        boxes = [(0, length, 0, LANES), (0, length, LANES, LANES), (0, 2 * third, 2 * LANES, LANES), (2 * third, third, 2 * LANES, LANES), (0, length, 3 * LANES, LANES)]
        parts = [Part(box, bits) for box in boxes[:4]] + [Part(boxes[4], far)]
        steps = [(0, -1), (4, -1), (1, -1), (2, -1), (0, 0), (3, -1), (4, 0), (1, 0), (0, 1), (4, 1), (2, 0), (1, 1), (3, 0), (2, 1), (3, 1), (0, 2), (1, 2), (2, 2), (4, 2), (3, 2)]
    else:
        parts = [Part((0, length, LANES * at, LANES), far if at == 1 else bits) for at in range(count)]
        steps = [(at, wave - at - 1) for wave in range(count + len(bits)) for at in range(count) if -1 <= wave - at - 1 < len(bits)]
    return parts, steps


def across(x, bit):
    count = lax.axis_size("tp")
    return lax.ppermute(x, "tp", [(i, i ^ (1 << bit)) for i in range(count)])


def after(x, axis):
    count = lax.axis_size(axis)
    return lax.ppermute(x, axis, [(i, i + 1) for i in range(count - 1)])


def later_rounds(message, inner_end, streams, taps, decay, init_state):
    first = lax.axis_index("ctx") == 0
    poles = decay.shape[0]
    tap_count = taps.shape[1]
    lag = tap_count - 1
    length = streams.shape[2]
    rims = message[poles:].reshape(3, PAD, -1)
    joined = jnp.concatenate([rims, streams[:, 0, :PAD].astype(F32)], axis=1)
    featured = sum(taps[:, i][:, None, :] * joined[:, PAD - i : 2 * PAD - i, :] for i in range(tap_count))
    head = jnp.where(first, 0.0, featured[1] * featured[2])
    local = jnp.where(first, 0.0, inner_end)

    def one(_, incoming):
        state = jnp.where(first, init_state[0], incoming)
        for j in range(lag):
            state = decay * state + head[j][None]
        ended = jnp.where(first, inner_end, local + power(decay, length - lag) * state)
        return after(ended, "ctx")

    state = lax.fori_loop(0, lax.axis_size("ctx") - 2, one, message[:poles])
    return jnp.concatenate([state, message[poles:]], axis=0)


def per_device(streams, taps, decay, residues, init_state, out_weight):
    length, channels = streams.shape[2:]
    poles = decay.shape[0]
    tiles = channels // LANES
    seg_len, turn = segments(length)
    peers = lax.axis_size("tp")
    width = out_weight.shape[1] // peers
    me = lax.axis_index("tp")
    where = jnp.stack([lax.axis_index("ctx"), me & 1, me >> 1]).astype(jnp.int32)
    rows = poles + 3 * PAD
    streams_hbm, weight_hbm = in_hbm(streams), in_hbm(out_weight)
    split = (tiles, seg_len, SEGS, LANES)
    driven, inner, message, sent = pl.pallas_call(
        driven_kernel,
        out_shape=(
            jax.ShapeDtypeStruct(split, F32),
            jax.ShapeDtypeStruct((tiles, poles, SEGS, LANES), F32),
            jax.ShapeDtypeStruct((rows, channels), F32),
            jax.ShapeDtypeStruct((peers // 2, channels, width), BF16),
        ),
        in_specs=[SMEM, HBM, HBM, HBM, HBM, HBM],
        out_specs=(VMEM, VMEM, VMEM, VMEM),
        scratch_shapes=[
            pltpu.VMEM((2, EDGE + length, LANES), F32),
            pltpu.VMEM((tiles, 2, length, LANES), BF16),
            pltpu.VMEM((3, 16, channels), BF16),
            pltpu.VMEM(taps.shape, F32),
            pltpu.VMEM(decay.shape, F32),
            pltpu.VMEM(init_state.shape, F32),
            pltpu.SemaphoreType.DMA((peers // 2,)),
            pltpu.SemaphoreType.DMA((4 + tiles,)),
        ],
        compiler_params=pltpu.CompilerParams(vmem_limit_bytes=LIMIT),
        cost_estimate=QUICK,
        name="driven",
    )(where, streams_hbm, in_hbm(taps), in_hbm(decay), in_hbm(init_state), weight_hbm)
    passed = after(message, "ctx")
    swapped = across(sent, 0)
    response, query, mine = pl.pallas_call(
        response_kernel,
        out_shape=(
            jax.ShapeDtypeStruct(split, F32),
            jax.ShapeDtypeStruct(split, F32),
            jax.ShapeDtypeStruct((peers // 2, channels, width), BF16),
        ),
        in_specs=[SMEM] + [VMEM] * 6 + [HBM],
        out_specs=(VMEM, VMEM, VMEM),
        scratch_shapes=[pltpu.VMEM((EDGE + length, LANES), F32), pltpu.SemaphoreType.DMA((peers // 2,))],
        compiler_params=pltpu.CompilerParams(vmem_limit_bytes=LIMIT),
        cost_estimate=QUICK,
        name="response",
    )(where, streams, taps, decay, residues, driven, inner, weight_hbm)
    if lax.axis_size("ctx") > 2:
        passed = later_rounds(passed, message[:poles], streams, taps, decay, init_state)
    gated = pl.pallas_call(
        gated_kernel,
        out_shape=jax.ShapeDtypeStruct((length, channels), BF16),
        in_specs=[SMEM] + [VMEM] * 8,
        out_specs=VMEM,
        scratch_shapes=[
            pltpu.VMEM((PAD + 16, channels), F32),
            pltpu.VMEM((2 * poles, channels), F32),
            pltpu.VMEM((PAD + length, LANES), F32),
        ],
        compiler_params=pltpu.CompilerParams(vmem_limit_bytes=LIMIT),
        cost_estimate=QUICK,
        name="gated",
    )(where, passed, streams, taps, decay, residues, init_state, response, query)
    other = across(gated, 0)

    parts, steps = plan(peers, length, width)
    flying, kept, finished, ordered = {}, {}, {}, gated
    for at, stage in steps:
        part = parts[at]
        if stage < 0:
            send, kept[at] = project(part, where, gated, other, mine, swapped, ordered)
            ordered = send
        elif stage + 1 < len(part.order):
            send, kept[at] = merge(kept[at], flying[at], ordered)
            ordered = send
        elif len(finished) + 1 < len(parts):
            ordered = finished[at] = finish(kept[at], flying[at], ordered)
            continue
        else:
            boxes = [parts[done].box for done in finished] + [part.box]
            return gather(list(finished.values()), boxes, kept[at], flying[at], ordered, length, width)
        flying[at] = across(send, part.order[stage + 1])


def solution(mesh):
    in_specs = (
        P(None, None, "ctx", "tp"),
        P(None, None, "tp"),
        P(None, "tp"),
        P(None, "tp"),
        P(None, None, "tp"),
        P("tp", None),
    )
    out_specs = P(None, "ctx", "tp")
    return jax.shard_map(
        per_device, mesh=mesh, in_specs=in_specs, out_specs=out_specs, check_vma=False
    )
```

```python
import dataclasses
import functools

import jax
import jax.numpy as jnp
from jax import lax
from jax.experimental import pallas as pl
from jax.experimental.pallas import tpu as pltpu
from jax.sharding import PartitionSpec as P

F32 = jnp.float32
BF16 = jnp.bfloat16
LANES = 128
SEGS = 8
PAD = 8
EDGE = 2 * PAD


def power(base, exponent):
    result, square = None, base
    while exponent:
        if exponent & 1:
            result = square if result is None else result * square
        exponent >>= 1
        if exponent:
            square = square * square
    return result


def segments(length):
    seg_len = (length + PAD) // SEGS
    return seg_len, next(n for n in (7, 8, 6, 5, 4, 3, 2, 1) if seg_len % n == 0)


def tree_sum(terms):
    while len(terms) > 1:
        paired = [a + b for a, b in zip(terms[::2], terms[1::2])]
        terms = paired + terms[len(paired) * 2 :]
    return terms[0]


def weight_columns(weight_hbm, ref, side, sems):
    parts, _, width = ref.shape
    copies = []
    for part in range(parts):
        column = pl.multiple_of((2 * part + side) * width, LANES)
        copies.append(pltpu.make_async_copy(weight_hbm.at[:, pl.ds(column, width)], ref.at[part], sems.at[part]))
    for copy in copies:
        copy.start()
    return copies


def driven_kernel(where_ref, streams_hbm, taps_hbm, decay_hbm, init_hbm, weight_hbm, driven_ref, inner_ref, message_ref, sent_ref, wide_ref, streams_ref, rim_ref, taps_ref, decay_ref, init_ref, weight_sems, sems):
    first = where_ref[0] == 0
    core = where_ref[1]
    poles = decay_ref.shape[0]
    tap_count = taps_ref.shape[1]
    length, channels = streams_hbm.shape[2:]
    tiles = channels // LANES
    seg_len, turn = segments(length)
    small = [
        pltpu.make_async_copy(taps_hbm, taps_ref, sems.at[0]),
        pltpu.make_async_copy(decay_hbm, decay_ref, sems.at[1]),
        pltpu.make_async_copy(init_hbm, init_ref, sems.at[2]),
        pltpu.make_async_copy(streams_hbm.at[:, 0, length - 16 :], rim_ref, sems.at[3]),
    ]
    loads = []
    for tile in range(tiles):
        lanes = pl.ds(tile * LANES, LANES)
        loads.append(pltpu.make_async_copy(streams_hbm.at[1:3, 0, :, lanes], streams_ref.at[tile], sems.at[4 + tile]))
    loads[0].start()
    for copy in small + loads[1:]:
        copy.start()
    copies = weight_columns(weight_hbm, sent_ref, 1 - core, weight_sems)
    for copy in small:
        copy.wait()
    sublane = lax.broadcasted_iota(jnp.int32, (SEGS, LANES), 0)
    for tile in range(tiles):
        lanes = slice(tile * LANES, (tile + 1) * LANES)
        loads[tile].wait()
        for s in range(2):
            wide_ref[s, 0:EDGE, :] = jnp.zeros((EDGE, LANES), F32)
            wide_ref[s, EDGE : EDGE + length, :] = streams_ref[tile, s].astype(F32)
        taps = [[jnp.broadcast_to(taps_ref[1 + s, i : i + 1, lanes], (SEGS, LANES)) for i in range(tap_count)] for s in range(2)]

        def row(s, j):
            return wide_ref[s, pl.ds(PAD + j, SEGS, stride=seg_len), :]

        def block(base, windows):
            windows = list(windows)
            for step in range(turn):
                made = []
                for s in range(2):
                    seen = list(windows[s]) + [row(s, base + step)]
                    made.append(tree_sum([taps[s][i] * seen[-1 - i] for i in range(tap_count)]))
                    windows[s] = tuple(seen[1:])
                driven_ref[tile, base + step] = made[0] * made[1]
            return tuple(windows)

        windows = tuple(tuple(row(s, j - (tap_count - 1)) for j in range(tap_count - 1)) for s in range(2))
        lax.fori_loop(0, seg_len // turn, lambda b, w: block(b * turn, w), windows)
        for j in range(tap_count - 1):
            driven_ref[tile, PAD + j, 0:1, :] = jnp.where(first, driven_ref[tile, PAD + j, 0:1, :], 0.0)

        decays = [jnp.broadcast_to(decay_ref[n : n + 1, lanes], (SEGS, LANES)) for n in range(poles)]

        def scan(b, states):
            states = list(states)
            for step in range(turn):
                value = driven_ref[tile, b * turn + step]
                states = [d * s + value for d, s in zip(decays, states)]
            return tuple(states)

        zero = jnp.zeros((SEGS, LANES), F32)
        ends = lax.fori_loop(0, seg_len // turn, scan, (zero,) * poles)
        for n in range(poles):
            total, factor = ends[n], power(decays[n], seg_len)
            for reach in (1, 2, 4):
                moved = jnp.where(sublane >= reach, pltpu.roll(total, reach, 0), 0.0)
                total = total + factor * moved
                factor = factor * factor
            inner_ref[tile, n] = total
            message_ref[n : n + 1, lanes] = total[SEGS - 1 : SEGS, :]
    carried = power(decay_ref[...], length) * init_ref[0]
    message_ref[0:poles, :] = message_ref[0:poles, :] + jnp.where(first, carried, 0.0)
    for s in range(3):
        message_ref[poles + s * PAD : poles + (s + 1) * PAD, :] = rim_ref[s].astype(F32)[16 - PAD :]
    for copy in copies:
        copy.wait()


def response_kernel(where_ref, query_in_ref, taps_ref, decay_ref, residues_ref, driven_ref, inner_ref, weight_hbm, response_ref, query_ref, mine_ref, wide_ref, weight_sems):
    poles = decay_ref.shape[0]
    tap_count = taps_ref.shape[1]
    lag = tap_count - 1
    length, channels = query_in_ref.shape[2:]
    tiles = channels // LANES
    seg_len, turn = segments(length)
    copies = weight_columns(weight_hbm, mine_ref, where_ref[1], weight_sems)
    sublane = lax.broadcasted_iota(jnp.int32, (SEGS, LANES), 0)
    for tile in range(tiles):
        lanes = slice(tile * LANES, (tile + 1) * LANES)
        wide_ref[0:EDGE, :] = jnp.zeros((EDGE, LANES), F32)
        wide_ref[EDGE : EDGE + length, :] = query_in_ref[0, 0, :, lanes].astype(F32)
        taps = [jnp.broadcast_to(taps_ref[0, i : i + 1, lanes], (SEGS, LANES)) for i in range(tap_count)]

        def row(j):
            return wide_ref[pl.ds(PAD + j, SEGS, stride=seg_len), :]

        def fir(b, window):
            window = list(window)
            for step in range(turn):
                window.append(row(b * turn + step))
                query_ref[tile, b * turn + step] = tree_sum([taps[i] * window[-1 - i] for i in range(tap_count)])
                window = window[1:]
            return tuple(window)

        lax.fori_loop(0, seg_len // turn, fir, tuple(row(j - lag) for j in range(lag)))

        decays = [jnp.broadcast_to(decay_ref[n : n + 1, lanes], (SEGS, LANES)) for n in range(poles)]
        weights = [jnp.broadcast_to(residues_ref[n : n + 1, lanes], (SEGS, LANES)) for n in range(poles)]
        states = [jnp.where(sublane == 0, 0.0, pltpu.roll(inner_ref[tile, n], 1, 0)) for n in range(poles)]

        def scan(b, states):
            states = list(states)
            for step in range(turn):
                value = driven_ref[tile, b * turn + step]
                states = [d * s + value for d, s in zip(decays, states)]
                response_ref[tile, b * turn + step] = tree_sum([r * s for r, s in zip(weights, states)])
            return tuple(states)

        lax.fori_loop(0, seg_len // turn, scan, tuple(states))
    for copy in copies:
        copy.wait()


def gated_kernel(where_ref, message_ref, head_in_ref, taps_ref, decay_ref, residues_ref, init_ref, response_ref, query_ref, gated_ref, head_ref, start_ref, out_ref, early_ref):
    first = where_ref[0] == 0
    poles = decay_ref.shape[0]
    tap_count = taps_ref.shape[1]
    lag = tap_count - 1
    length, channels = gated_ref.shape
    tiles = channels // LANES
    seg_len, turn = segments(length)
    sublane = lax.broadcasted_iota(jnp.int32, (SEGS, LANES), 0)

    heads = []
    for s in range(3):
        head_ref[0:PAD, :] = jnp.where(first, 0.0, message_ref[poles + s * PAD : poles + (s + 1) * PAD, :])
        head_ref[PAD : PAD + 16, :] = head_in_ref[s, 0, 0:16, :].astype(F32)
        heads.append(tree_sum([taps_ref[s, i : i + 1, :] * head_ref[PAD - i : 2 * PAD - i, :] for i in range(tap_count)]))
    head_query = heads[0]
    counted = jnp.where(first, 0.0, heads[1] * heads[2])
    decay, residues = decay_ref[...], residues_ref[...]
    state = jnp.where(first, init_ref[0], message_ref[0:poles, :])
    for j in range(lag):
        state = decay * state + counted[j : j + 1, :]
        early_ref[j : j + 1, :] = jnp.sum(residues * state, axis=0, keepdims=True)
    state = state * residues
    start_ref[0:poles, :] = state / power(decay, PAD + lag)
    start_ref[poles:, :] = state * power(decay, seg_len - PAD - lag)

    for tile in range(tiles):
        lanes = slice(tile * LANES, (tile + 1) * LANES)
        decays = [jnp.broadcast_to(decay_ref[n : n + 1, lanes], (SEGS, LANES)) for n in range(poles)]
        states = []
        for n in range(poles):
            factor = power(decays[n], seg_len)
            spread = jnp.broadcast_to(start_ref[poles + n : poles + n + 1, lanes], (SEGS, LANES))
            before = sublane - 1
            for bit in (1, 2, 4):
                spread = jnp.where(jnp.bitwise_and(before, bit) != 0, spread * factor, spread)
                factor = factor * factor
            own = jnp.broadcast_to(start_ref[n : n + 1, lanes], (SEGS, LANES))
            states.append(jnp.where(sublane == 0, own, spread))

        def block(b, states):
            states = list(states)
            for step in range(turn):
                at = b * turn + step
                states = [d * s for d, s in zip(decays, states)]
                total = response_ref[tile, at] + tree_sum(states)
                out_ref[pl.ds(at, SEGS, stride=seg_len), :] = total * query_ref[tile, at]
            return tuple(states)

        lax.fori_loop(0, seg_len // turn, block, tuple(states))
        for j in range(lag):
            total = response_ref[tile, PAD + j, 0:1, :] + early_ref[j : j + 1, lanes]
            out_ref[PAD + j : PAD + j + 1, :] = total * head_query[j : j + 1, lanes]
        gated_ref[:, lanes] = out_ref[PAD:, :].astype(BF16)


def relative(index, high, order):
    value = high << (order[0] - 1)
    count = len(order) - 1
    for place, bit in enumerate(order[1:]):
        value = value | (((index >> (count - 1 - place)) & 1) << (bit - 1))
    return value


def sides(part, where_ref, weight_ref, index):
    _, _, column, columns = part.box
    blocks = [relative(index, high, part.order) ^ where_ref[2] for high in (1, 0)]
    return jnp.concatenate([weight_ref[block, :, column : column + columns] for block in blocks], axis=1)


def project_kernel(part, where_ref, own_ref, other_ref, mine_ref, theirs_ref, order_ref, send_ref, keep_ref):
    row, rows, _, columns = part.box
    wide = jnp.concatenate([own_ref[row : row + rows, :], other_ref[row : row + rows, :]], axis=1)

    def step(index):
        both = jnp.concatenate([sides(part, where_ref, ref, index) for ref in (mine_ref, theirs_ref)], axis=0)
        total = jnp.dot(wide, both, preferred_element_type=F32)
        send_ref[index] = total[:, :columns].astype(BF16)
        keep_ref[index] = total[:, columns:]

    for index in range(send_ref.shape[0]):
        step(index)


def project_own_kernel(part, where_ref, own_ref, mine_ref, out_ref):
    row, rows, _, _ = part.box

    def step(index):
        out_ref[index] = jnp.dot(own_ref[row : row + rows, :], sides(part, where_ref, mine_ref, index), preferred_element_type=F32)

    for index in range(out_ref.shape[0]):
        step(index)


def project_other_kernel(part, where_ref, sum_ref, other_ref, theirs_ref, send_ref, keep_ref):
    row, rows, _, columns = part.box

    def step(index):
        total = sum_ref[index] + jnp.dot(other_ref[row : row + rows, :], sides(part, where_ref, theirs_ref, index), preferred_element_type=F32)
        send_ref[index] = total[:, :columns].astype(BF16)
        keep_ref[index] = total[:, columns:]

    for index in range(send_ref.shape[0]):
        step(index)


def merge_kernel(keep_ref, received_ref, order_ref, send_ref, kept_ref):
    half = kept_ref.shape[0]
    send_ref[...] = (keep_ref[half:] + received_ref[half:].astype(F32)).astype(BF16)
    kept_ref[...] = keep_ref[:half] + received_ref[:half].astype(F32)


def finish_kernel(keep_ref, received_ref, order_ref, out_ref):
    out_ref[...] = (keep_ref[0] + received_ref[0].astype(F32)).astype(BF16)


def gather_kernel(boxes, *refs):
    count = len(boxes) - 1
    pieces, (keep_ref, received_ref, order_ref, out_ref, last_ref, sems) = refs[:count], refs[count:]
    copies = []
    for at, (piece, (row, rows, column, columns)) in enumerate(zip(list(pieces) + [last_ref], boxes)):
        if at == count:
            last_ref[...] = (keep_ref[0] + received_ref[0].astype(F32)).astype(BF16)
        place = out_ref.at[0, pl.ds(row, rows), pl.ds(column, columns)]
        copies.append(pltpu.make_async_copy(piece, place, sems.at[at]))
        copies[-1].start()
    for copy in copies:
        copy.wait()


SMEM = pl.BlockSpec(memory_space=pltpu.SMEM)
VMEM = pl.BlockSpec(memory_space=pltpu.VMEM)
HBM = pl.BlockSpec(memory_space=pltpu.HBM)
ANYWHERE = pl.BlockSpec(memory_space=pl.ANY)
LIMIT = 24 * 1024 * 1024
QUICK = pl.CostEstimate(flops=1, bytes_accessed=1, transcendentals=0)


def in_hbm(x):
    return pltpu.with_memory_space_constraint(x, pltpu.MemorySpace.HBM)


@dataclasses.dataclass(frozen=True)
class Part:
    box: tuple
    order: tuple


def project(part, where, own, other, mine, theirs, ordered):
    channels = own.shape[1]
    halves = mine.shape[0]
    rest = halves // 2
    _, rows, _, columns = part.box
    return pl.pallas_call(
        functools.partial(project_kernel, part),
        out_shape=(jax.ShapeDtypeStruct((rest, rows, columns), BF16), jax.ShapeDtypeStruct((rest, rows, columns), F32)),
        in_specs=[SMEM, VMEM, VMEM, VMEM, VMEM, ANYWHERE],
        out_specs=(VMEM, VMEM),
        compiler_params=pltpu.CompilerParams(vmem_limit_bytes=LIMIT),
        cost_estimate=QUICK,
        name="project",
    )(where, own, other, mine, theirs, ordered)


def project_own(part, where, own, mine):
    _, rows, _, columns = part.box
    return pl.pallas_call(
        functools.partial(project_own_kernel, part),
        out_shape=jax.ShapeDtypeStruct((mine.shape[0] // 2, rows, 2 * columns), F32),
        in_specs=[SMEM, VMEM, VMEM],
        out_specs=VMEM,
        compiler_params=pltpu.CompilerParams(vmem_limit_bytes=LIMIT),
        cost_estimate=QUICK,
        name="project_own",
    )(where, own, mine)


def project_other(part, where, total, other, theirs):
    _, rows, _, columns = part.box
    shape = (total.shape[0], rows, columns)
    return pl.pallas_call(
        functools.partial(project_other_kernel, part),
        out_shape=(jax.ShapeDtypeStruct(shape, BF16), jax.ShapeDtypeStruct(shape, F32)),
        in_specs=[SMEM, VMEM, VMEM, VMEM],
        out_specs=(VMEM, VMEM),
        compiler_params=pltpu.CompilerParams(vmem_limit_bytes=LIMIT),
        cost_estimate=QUICK,
        name="project_other",
    )(where, total, other, theirs)


def merge(keep, received, ordered):
    half = keep.shape[0] // 2
    shape = (half,) + keep.shape[1:]
    return pl.pallas_call(
        merge_kernel,
        out_shape=(jax.ShapeDtypeStruct(shape, BF16), jax.ShapeDtypeStruct(shape, F32)),
        in_specs=[VMEM, VMEM, ANYWHERE],
        out_specs=(VMEM, VMEM),
        compiler_params=pltpu.CompilerParams(vmem_limit_bytes=LIMIT),
        cost_estimate=QUICK,
        name="merge",
    )(keep, received, ordered)


def finish(keep, received, ordered):
    return pl.pallas_call(
        finish_kernel,
        out_shape=jax.ShapeDtypeStruct(keep.shape[1:], BF16),
        in_specs=[VMEM, VMEM, ANYWHERE],
        out_specs=VMEM,
        compiler_params=pltpu.CompilerParams(vmem_limit_bytes=LIMIT),
        cost_estimate=QUICK,
        name="finish",
    )(keep, received, ordered)


def gather(pieces, boxes, keep, received, ordered, length, width):
    return pl.pallas_call(
        functools.partial(gather_kernel, boxes),
        out_shape=jax.ShapeDtypeStruct((1, length, width), BF16),
        in_specs=[VMEM] * len(pieces) + [VMEM, VMEM, ANYWHERE],
        out_specs=HBM,
        scratch_shapes=[pltpu.VMEM(keep.shape[1:], BF16), pltpu.SemaphoreType.DMA((len(boxes),))],
        compiler_params=pltpu.CompilerParams(vmem_limit_bytes=LIMIT),
        cost_estimate=QUICK,
        name="gather",
    )(*pieces, keep, received, ordered)


def plan(peers, length, width):
    bits = tuple(range(1, peers.bit_length() - 1))
    far = bits[-2:] + bits[:-2]
    count = width // LANES
    if count == 4 and len(bits) == 3 and length % 48 == 0:
        third = length // 3
        boxes = [(0, length, 0, LANES), (0, length, 2 * LANES, LANES), (0, 2 * third, 3 * LANES, LANES), (2 * third, third, 3 * LANES, LANES), (0, length, LANES, LANES)]
        parts = [Part(box, bits) for box in boxes[:4]] + [Part(boxes[4], far)]
        steps = [(0, -1), (4, -1), (1, -1), (2, -1), (0, 0), (3, -1), (4, 0), (1, 0), (0, 1), (4, 1), (2, 0), (1, 1), (3, 0), (2, 1), (3, 1), (0, 2), (1, 2), (2, 2), (4, 2), (3, 2)]
    else:
        parts = [Part((0, length, LANES * at, LANES), far if at == 1 else bits) for at in range(count)]
        steps = [(at, wave - at - 1) for wave in range(count + len(bits)) for at in range(count) if -1 <= wave - at - 1 < len(bits)]
    return parts, steps


def across(x, bit):
    count = lax.axis_size("tp")
    return lax.ppermute(x, "tp", [(i, i ^ (1 << bit)) for i in range(count)])


def after(x, axis):
    count = lax.axis_size(axis)
    return lax.ppermute(x, axis, [(i, (i + 1) % count) for i in range(count)])


def later_rounds(message, inner_end, streams, taps, decay, init_state):
    first = lax.axis_index("ctx") == 0
    poles = decay.shape[0]
    tap_count = taps.shape[1]
    lag = tap_count - 1
    length = streams.shape[2]
    rims = message[poles:].reshape(3, PAD, -1)
    joined = jnp.concatenate([rims, streams[:, 0, :PAD].astype(F32)], axis=1)
    featured = sum(taps[:, i][:, None, :] * joined[:, PAD - i : 2 * PAD - i, :] for i in range(tap_count))
    head = jnp.where(first, 0.0, featured[1] * featured[2])
    local = jnp.where(first, 0.0, inner_end)

    def one(_, incoming):
        state = jnp.where(first, init_state[0], incoming)
        for j in range(lag):
            state = decay * state + head[j][None]
        ended = jnp.where(first, inner_end, local + power(decay, length - lag) * state)
        return after(ended, "ctx")

    state = lax.fori_loop(0, lax.axis_size("ctx") - 2, one, message[:poles])
    return jnp.concatenate([state, message[poles:]], axis=0)


def per_device(streams, taps, decay, residues, init_state, out_weight):
    length, channels = streams.shape[2:]
    poles = decay.shape[0]
    tiles = channels // LANES
    seg_len, turn = segments(length)
    peers = lax.axis_size("tp")
    width = out_weight.shape[1] // peers
    me = lax.axis_index("tp")
    where = jnp.stack([lax.axis_index("ctx"), me & 1, me >> 1]).astype(jnp.int32)
    rows = poles + 3 * PAD
    streams_hbm, weight_hbm = in_hbm(streams), in_hbm(out_weight)
    split = (tiles, seg_len, SEGS, LANES)
    columns = jax.ShapeDtypeStruct((peers // 2, channels, width), BF16)
    driven, inner, message, sent = pl.pallas_call(
        driven_kernel,
        out_shape=(
            jax.ShapeDtypeStruct(split, F32),
            jax.ShapeDtypeStruct((tiles, poles, SEGS, LANES), F32),
            jax.ShapeDtypeStruct((rows, channels), F32),
            columns,
        ),
        in_specs=[SMEM, HBM, HBM, HBM, HBM, HBM],
        out_specs=(VMEM, VMEM, VMEM, VMEM),
        scratch_shapes=[
            pltpu.VMEM((2, EDGE + length, LANES), F32),
            pltpu.VMEM((tiles, 2, length, LANES), BF16),
            pltpu.VMEM((3, 16, channels), BF16),
            pltpu.VMEM(taps.shape, F32),
            pltpu.VMEM(decay.shape, F32),
            pltpu.VMEM(init_state.shape, F32),
            pltpu.SemaphoreType.DMA((peers // 2,)),
            pltpu.SemaphoreType.DMA((4 + tiles,)),
        ],
        compiler_params=pltpu.CompilerParams(vmem_limit_bytes=LIMIT),
        cost_estimate=QUICK,
        name="driven",
    )(where, streams_hbm, in_hbm(taps), in_hbm(decay), in_hbm(init_state), weight_hbm)
    passed = after(message, "ctx")
    theirs = across(sent, 0)
    response, query, mine = pl.pallas_call(
        response_kernel,
        out_shape=(
            jax.ShapeDtypeStruct(split, F32),
            jax.ShapeDtypeStruct(split, F32),
            columns,
        ),
        in_specs=[SMEM] + [VMEM] * 6 + [HBM],
        out_specs=(VMEM, VMEM, VMEM),
        scratch_shapes=[pltpu.VMEM((EDGE + length, LANES), F32), pltpu.SemaphoreType.DMA((peers // 2,))],
        compiler_params=pltpu.CompilerParams(vmem_limit_bytes=LIMIT),
        cost_estimate=QUICK,
        name="response",
    )(where, streams, taps, decay, residues, driven, inner, weight_hbm)
    if lax.axis_size("ctx") > 2:
        passed = later_rounds(passed, message[:poles], streams, taps, decay, init_state)
    gated = pl.pallas_call(
        gated_kernel,
        out_shape=jax.ShapeDtypeStruct((length, channels), BF16),
        in_specs=[SMEM] + [VMEM] * 8,
        out_specs=VMEM,
        scratch_shapes=[
            pltpu.VMEM((PAD + 16, channels), F32),
            pltpu.VMEM((2 * poles, channels), F32),
            pltpu.VMEM((PAD + length, LANES), F32),
            pltpu.VMEM((PAD, channels), F32),
        ],
        compiler_params=pltpu.CompilerParams(vmem_limit_bytes=LIMIT),
        cost_estimate=QUICK,
        name="gated",
    )(where, passed, streams, taps, decay, residues, init_state, response, query)
    other = across(gated, 0)

    parts, steps = plan(peers, length, width)
    flying, kept, finished, ordered = {}, {}, {}, gated
    started = project_own(parts[steps[0][0]], where, gated, mine)
    for at, stage in steps:
        part = parts[at]
        if stage < 0:
            if at == steps[0][0]:
                send, kept[at] = project_other(part, where, started, other, theirs)
            else:
                send, kept[at] = project(part, where, gated, other, mine, theirs, ordered)
            ordered = send
        elif stage + 1 < len(part.order):
            send, kept[at] = merge(kept[at], flying[at], ordered)
            ordered = send
        elif len(finished) + 1 < len(parts):
            ordered = finished[at] = finish(kept[at], flying[at], ordered)
            continue
        else:
            boxes = [parts[done].box for done in finished] + [part.box]
            return gather(list(finished.values()), boxes, kept[at], flying[at], ordered, length, width)
        flying[at] = across(send, part.order[stage + 1])


def solution(mesh):
    in_specs = (
        P(None, None, "ctx", "tp"),
        P(None, None, "tp"),
        P(None, "tp"),
        P(None, "tp"),
        P(None, None, "tp"),
        P("tp", None),
    )
    out_specs = P(None, "ctx", "tp")
    return jax.shard_map(
        per_device, mesh=mesh, in_specs=in_specs, out_specs=out_specs, check_vma=False
    )
```

```python
import dataclasses
import functools

import jax
import jax.numpy as jnp
from jax import lax
from jax.experimental import pallas as pl
from jax.experimental.pallas import tpu as pltpu
from jax.sharding import PartitionSpec as P

F32 = jnp.float32
BF16 = jnp.bfloat16
LANES = 128
SEGS = 8
PAD = 8
EDGE = 2 * PAD


def power(base, exponent):
    result, square = None, base
    while exponent:
        if exponent & 1:
            result = square if result is None else result * square
        exponent >>= 1
        if exponent:
            square = square * square
    return result


def segments(length):
    seg_len = (length + PAD) // SEGS
    return seg_len, next(n for n in (7, 8, 6, 5, 4, 3, 2, 1) if seg_len % n == 0)


def tree_sum(terms):
    while len(terms) > 1:
        paired = [a + b for a, b in zip(terms[::2], terms[1::2])]
        terms = paired + terms[len(paired) * 2 :]
    return terms[0]


def weight_columns(weight_hbm, ref, side, sems):
    parts, _, width = ref.shape
    copies = []
    for part in range(parts):
        column = pl.multiple_of((2 * part + side) * width, LANES)
        copies.append(pltpu.make_async_copy(weight_hbm.at[:, pl.ds(column, width)], ref.at[part], sems.at[part]))
    return copies


def driven_kernel(where_ref, streams_hbm, taps_hbm, decay_hbm, init_hbm, weight_hbm, driven_ref, inner_ref, message_ref, sent_ref, wide_ref, streams_ref, rim_ref, taps_ref, decay_ref, init_ref, weight_sems, sems):
    first = where_ref[0] == 0
    core = where_ref[1]
    poles = decay_ref.shape[0]
    tap_count = taps_ref.shape[1]
    length, channels = streams_hbm.shape[2:]
    tiles = channels // LANES
    seg_len, turn = segments(length)
    small = [
        pltpu.make_async_copy(taps_hbm, taps_ref, sems.at[0]),
        pltpu.make_async_copy(decay_hbm, decay_ref, sems.at[1]),
        pltpu.make_async_copy(init_hbm, init_ref, sems.at[2]),
        pltpu.make_async_copy(streams_hbm.at[:, 0, length - 16 :], rim_ref, sems.at[3]),
    ]
    loads = []
    for tile in range(tiles):
        lanes = pl.ds(tile * LANES, LANES)
        loads.append(pltpu.make_async_copy(streams_hbm.at[1:3, 0, :, lanes], streams_ref.at[tile], sems.at[4 + tile]))
    loads[0].start()
    for copy in small + loads[1:]:
        copy.start()
    copies = weight_columns(weight_hbm, sent_ref, 1 - core, weight_sems)
    for copy in small:
        copy.wait()
    sublane = lax.broadcasted_iota(jnp.int32, (SEGS, LANES), 0)
    for tile in range(tiles):
        lanes = slice(tile * LANES, (tile + 1) * LANES)
        loads[tile].wait()
        if tile < 2:
            for copy in copies[tile::2]:
                copy.start()
        for s in range(2):
            wide_ref[s, 0:EDGE, :] = jnp.zeros((EDGE, LANES), F32)
            wide_ref[s, EDGE : EDGE + length, :] = streams_ref[tile, s].astype(F32)
        taps = [[jnp.broadcast_to(taps_ref[1 + s, i : i + 1, lanes], (SEGS, LANES)) for i in range(tap_count)] for s in range(2)]

        def row(s, j):
            return wide_ref[s, pl.ds(PAD + j, SEGS, stride=seg_len), :]

        def block(base, windows):
            windows = list(windows)
            for step in range(turn):
                made = []
                for s in range(2):
                    seen = list(windows[s]) + [row(s, base + step)]
                    made.append(tree_sum([taps[s][i] * seen[-1 - i] for i in range(tap_count)]))
                    windows[s] = tuple(seen[1:])
                driven_ref[tile, base + step] = made[0] * made[1]
            return tuple(windows)

        windows = tuple(tuple(row(s, j - (tap_count - 1)) for j in range(tap_count - 1)) for s in range(2))
        lax.fori_loop(0, seg_len // turn, lambda b, w: block(b * turn, w), windows)
        for j in range(tap_count - 1):
            driven_ref[tile, PAD + j, 0:1, :] = jnp.where(first, driven_ref[tile, PAD + j, 0:1, :], 0.0)

        decays = [jnp.broadcast_to(decay_ref[n : n + 1, lanes], (SEGS, LANES)) for n in range(poles)]

        def scan(b, states):
            states = list(states)
            for step in range(turn):
                value = driven_ref[tile, b * turn + step]
                states = [d * s + value for d, s in zip(decays, states)]
            return tuple(states)

        zero = jnp.zeros((SEGS, LANES), F32)
        ends = lax.fori_loop(0, seg_len // turn, scan, (zero,) * poles)
        for n in range(poles):
            total, factor = ends[n], power(decays[n], seg_len)
            for reach in (1, 2, 4):
                moved = jnp.where(sublane >= reach, pltpu.roll(total, reach, 0), 0.0)
                total = total + factor * moved
                factor = factor * factor
            inner_ref[tile, n] = total
            message_ref[n : n + 1, lanes] = total[SEGS - 1 : SEGS, :]
    carried = power(decay_ref[...], length) * init_ref[0]
    message_ref[0:poles, :] = message_ref[0:poles, :] + jnp.where(first, carried, 0.0)
    for s in range(3):
        message_ref[poles + s * PAD : poles + (s + 1) * PAD, :] = rim_ref[s].astype(F32)[16 - PAD :]
    for copy in copies:
        copy.wait()


def response_kernel(where_ref, query_in_ref, taps_ref, decay_ref, residues_ref, driven_ref, inner_ref, weight_hbm, response_ref, query_ref, mine_ref, wide_ref, weight_sems):
    poles = decay_ref.shape[0]
    tap_count = taps_ref.shape[1]
    lag = tap_count - 1
    length, channels = query_in_ref.shape[2:]
    tiles = channels // LANES
    seg_len, turn = segments(length)
    copies = weight_columns(weight_hbm, mine_ref, where_ref[1], weight_sems)
    for copy in copies:
        copy.start()
    sublane = lax.broadcasted_iota(jnp.int32, (SEGS, LANES), 0)
    for tile in range(tiles):
        lanes = slice(tile * LANES, (tile + 1) * LANES)
        wide_ref[0:EDGE, :] = jnp.zeros((EDGE, LANES), F32)
        wide_ref[EDGE : EDGE + length, :] = query_in_ref[0, 0, :, lanes].astype(F32)
        taps = [jnp.broadcast_to(taps_ref[0, i : i + 1, lanes], (SEGS, LANES)) for i in range(tap_count)]

        def row(j):
            return wide_ref[pl.ds(PAD + j, SEGS, stride=seg_len), :]

        def fir(b, window):
            window = list(window)
            for step in range(turn):
                window.append(row(b * turn + step))
                query_ref[tile, b * turn + step] = tree_sum([taps[i] * window[-1 - i] for i in range(tap_count)])
                window = window[1:]
            return tuple(window)

        lax.fori_loop(0, seg_len // turn, fir, tuple(row(j - lag) for j in range(lag)))

        decays = [jnp.broadcast_to(decay_ref[n : n + 1, lanes], (SEGS, LANES)) for n in range(poles)]
        weights = [jnp.broadcast_to(residues_ref[n : n + 1, lanes], (SEGS, LANES)) for n in range(poles)]
        states = [jnp.where(sublane == 0, 0.0, pltpu.roll(inner_ref[tile, n], 1, 0)) for n in range(poles)]

        def scan(b, states):
            states = list(states)
            for step in range(turn):
                value = driven_ref[tile, b * turn + step]
                states = [d * s + value for d, s in zip(decays, states)]
                response_ref[tile, b * turn + step] = tree_sum([r * s for r, s in zip(weights, states)])
            return tuple(states)

        lax.fori_loop(0, seg_len // turn, scan, tuple(states))
    for copy in copies:
        copy.wait()


def gated_kernel(where_ref, message_ref, head_in_ref, taps_ref, decay_ref, residues_ref, init_ref, response_ref, query_ref, gated_ref, head_ref, start_ref, out_ref, early_ref):
    first = where_ref[0] == 0
    poles = decay_ref.shape[0]
    tap_count = taps_ref.shape[1]
    lag = tap_count - 1
    length, channels = gated_ref.shape
    tiles = channels // LANES
    seg_len, turn = segments(length)
    sublane = lax.broadcasted_iota(jnp.int32, (SEGS, LANES), 0)

    heads = []
    for s in range(3):
        head_ref[0:PAD, :] = jnp.where(first, 0.0, message_ref[poles + s * PAD : poles + (s + 1) * PAD, :])
        head_ref[PAD : PAD + 16, :] = head_in_ref[s, 0, 0:16, :].astype(F32)
        heads.append(tree_sum([taps_ref[s, i : i + 1, :] * head_ref[PAD - i : 2 * PAD - i, :] for i in range(tap_count)]))
    head_query = heads[0]
    counted = jnp.where(first, 0.0, heads[1] * heads[2])
    decay, residues = decay_ref[...], residues_ref[...]
    state = jnp.where(first, init_ref[0], message_ref[0:poles, :])
    for j in range(lag):
        state = decay * state + counted[j : j + 1, :]
        early_ref[j : j + 1, :] = jnp.sum(residues * state, axis=0, keepdims=True)
    state = state * residues
    start_ref[0:poles, :] = state / power(decay, PAD + lag)
    start_ref[poles:, :] = state * power(decay, seg_len - PAD - lag)

    for tile in range(tiles):
        lanes = slice(tile * LANES, (tile + 1) * LANES)
        decays = [jnp.broadcast_to(decay_ref[n : n + 1, lanes], (SEGS, LANES)) for n in range(poles)]
        states = []
        for n in range(poles):
            factor = power(decays[n], seg_len)
            spread = jnp.broadcast_to(start_ref[poles + n : poles + n + 1, lanes], (SEGS, LANES))
            before = sublane - 1
            for bit in (1, 2, 4):
                spread = jnp.where(jnp.bitwise_and(before, bit) != 0, spread * factor, spread)
                factor = factor * factor
            own = jnp.broadcast_to(start_ref[n : n + 1, lanes], (SEGS, LANES))
            states.append(jnp.where(sublane == 0, own, spread))

        def block(b, states):
            states = list(states)
            for step in range(turn):
                at = b * turn + step
                states = [d * s for d, s in zip(decays, states)]
                total = response_ref[tile, at] + tree_sum(states)
                out_ref[pl.ds(at, SEGS, stride=seg_len), :] = total * query_ref[tile, at]
            return tuple(states)

        lax.fori_loop(0, seg_len // turn, block, tuple(states))
        for j in range(lag):
            total = response_ref[tile, PAD + j, 0:1, :] + early_ref[j : j + 1, lanes]
            out_ref[PAD + j : PAD + j + 1, :] = total * head_query[j : j + 1, lanes]
        gated_ref[:, lanes] = out_ref[PAD:, :].astype(BF16)


def relative(index, high, order):
    value = high << (order[0] - 1)
    count = len(order) - 1
    for place, bit in enumerate(order[1:]):
        value = value | (((index >> (count - 1 - place)) & 1) << (bit - 1))
    return value


def sides(part, where_ref, weight_ref, index):
    _, _, column, columns = part.box
    blocks = [relative(index, high, part.order) ^ where_ref[2] for high in (1, 0)]
    return jnp.concatenate([weight_ref[block, :, column : column + columns] for block in blocks], axis=1)


def project_kernel(part, where_ref, own_ref, other_ref, mine_ref, theirs_ref, order_ref, send_ref, keep_ref):
    row, rows, _, columns = part.box
    wide = jnp.concatenate([own_ref[row : row + rows, :], other_ref[row : row + rows, :]], axis=1)

    def step(index):
        both = jnp.concatenate([sides(part, where_ref, ref, index) for ref in (mine_ref, theirs_ref)], axis=0)
        total = jnp.dot(wide, both, preferred_element_type=F32)
        send_ref[index] = total[:, :columns].astype(BF16)
        keep_ref[index] = total[:, columns:]

    for index in range(send_ref.shape[0]):
        step(index)


def project_own_kernel(part, where_ref, own_ref, mine_ref, out_ref):
    row, rows, _, _ = part.box

    def step(index):
        out_ref[index] = jnp.dot(own_ref[row : row + rows, :], sides(part, where_ref, mine_ref, index), preferred_element_type=F32)

    for index in range(out_ref.shape[0]):
        step(index)


def project_other_kernel(part, where_ref, sum_ref, other_ref, theirs_ref, send_ref, keep_ref):
    row, rows, _, columns = part.box

    def step(index):
        total = sum_ref[index] + jnp.dot(other_ref[row : row + rows, :], sides(part, where_ref, theirs_ref, index), preferred_element_type=F32)
        send_ref[index] = total[:, :columns].astype(BF16)
        keep_ref[index] = total[:, columns:]

    for index in range(send_ref.shape[0]):
        step(index)


def merge_kernel(keep_ref, received_ref, order_ref, send_ref, kept_ref):
    half = kept_ref.shape[0]
    send_ref[...] = (keep_ref[half:] + received_ref[half:].astype(F32)).astype(BF16)
    kept_ref[...] = keep_ref[:half] + received_ref[:half].astype(F32)


def finish_kernel(keep_ref, received_ref, order_ref, out_ref):
    out_ref[...] = (keep_ref[0] + received_ref[0].astype(F32)).astype(BF16)


def gather_kernel(boxes, *refs):
    count = len(boxes) - 1
    pieces, (keep_ref, received_ref, order_ref, out_ref, last_ref, sems) = refs[:count], refs[count:]
    copies = []
    for at, (piece, (row, rows, column, columns)) in enumerate(zip(list(pieces) + [last_ref], boxes)):
        if at == count:
            last_ref[...] = (keep_ref[0] + received_ref[0].astype(F32)).astype(BF16)
        place = out_ref.at[0, pl.ds(row, rows), pl.ds(column, columns)]
        copies.append(pltpu.make_async_copy(piece, place, sems.at[at]))
        copies[-1].start()
    for copy in copies:
        copy.wait()


SMEM = pl.BlockSpec(memory_space=pltpu.SMEM)
VMEM = pl.BlockSpec(memory_space=pltpu.VMEM)
HBM = pl.BlockSpec(memory_space=pltpu.HBM)
ANYWHERE = pl.BlockSpec(memory_space=pl.ANY)
LIMIT = 24 * 1024 * 1024
QUICK = pl.CostEstimate(flops=1, bytes_accessed=1, transcendentals=0)


def in_hbm(x):
    return pltpu.with_memory_space_constraint(x, pltpu.MemorySpace.HBM)


@dataclasses.dataclass(frozen=True)
class Part:
    box: tuple
    order: tuple


def project(part, where, own, other, mine, theirs, ordered):
    channels = own.shape[1]
    halves = mine.shape[0]
    rest = halves // 2
    _, rows, _, columns = part.box
    return pl.pallas_call(
        functools.partial(project_kernel, part),
        out_shape=(jax.ShapeDtypeStruct((rest, rows, columns), BF16), jax.ShapeDtypeStruct((rest, rows, columns), F32)),
        in_specs=[SMEM, VMEM, VMEM, VMEM, VMEM, ANYWHERE],
        out_specs=(VMEM, VMEM),
        compiler_params=pltpu.CompilerParams(vmem_limit_bytes=LIMIT),
        cost_estimate=QUICK,
        name="project",
    )(where, own, other, mine, theirs, ordered)


def project_own(part, where, own, mine):
    _, rows, _, columns = part.box
    return pl.pallas_call(
        functools.partial(project_own_kernel, part),
        out_shape=jax.ShapeDtypeStruct((mine.shape[0] // 2, rows, 2 * columns), F32),
        in_specs=[SMEM, VMEM, VMEM],
        out_specs=VMEM,
        compiler_params=pltpu.CompilerParams(vmem_limit_bytes=LIMIT),
        cost_estimate=QUICK,
        name="project_own",
    )(where, own, mine)


def project_other(part, where, total, other, theirs):
    _, rows, _, columns = part.box
    shape = (total.shape[0], rows, columns)
    return pl.pallas_call(
        functools.partial(project_other_kernel, part),
        out_shape=(jax.ShapeDtypeStruct(shape, BF16), jax.ShapeDtypeStruct(shape, F32)),
        in_specs=[SMEM, VMEM, VMEM, VMEM],
        out_specs=(VMEM, VMEM),
        compiler_params=pltpu.CompilerParams(vmem_limit_bytes=LIMIT),
        cost_estimate=QUICK,
        name="project_other",
    )(where, total, other, theirs)


def merge(keep, received, ordered):
    half = keep.shape[0] // 2
    shape = (half,) + keep.shape[1:]
    return pl.pallas_call(
        merge_kernel,
        out_shape=(jax.ShapeDtypeStruct(shape, BF16), jax.ShapeDtypeStruct(shape, F32)),
        in_specs=[VMEM, VMEM, ANYWHERE],
        out_specs=(VMEM, VMEM),
        compiler_params=pltpu.CompilerParams(vmem_limit_bytes=LIMIT),
        cost_estimate=QUICK,
        name="merge",
    )(keep, received, ordered)


def finish(keep, received, ordered):
    return pl.pallas_call(
        finish_kernel,
        out_shape=jax.ShapeDtypeStruct(keep.shape[1:], BF16),
        in_specs=[VMEM, VMEM, ANYWHERE],
        out_specs=VMEM,
        compiler_params=pltpu.CompilerParams(vmem_limit_bytes=LIMIT),
        cost_estimate=QUICK,
        name="finish",
    )(keep, received, ordered)


def gather(pieces, boxes, keep, received, ordered, length, width):
    return pl.pallas_call(
        functools.partial(gather_kernel, boxes),
        out_shape=jax.ShapeDtypeStruct((1, length, width), BF16),
        in_specs=[VMEM] * len(pieces) + [VMEM, VMEM, ANYWHERE],
        out_specs=HBM,
        scratch_shapes=[pltpu.VMEM(keep.shape[1:], BF16), pltpu.SemaphoreType.DMA((len(boxes),))],
        compiler_params=pltpu.CompilerParams(vmem_limit_bytes=LIMIT),
        cost_estimate=QUICK,
        name="gather",
    )(*pieces, keep, received, ordered)


def plan(peers, length, width):
    bits = tuple(range(1, peers.bit_length() - 1))
    far = bits[-2:] + bits[:-2]
    count = width // LANES
    if count == 4 and len(bits) == 3 and length % 48 == 0:
        third = length // 3
        boxes = [(0, length, 0, LANES), (0, length, 2 * LANES, LANES), (0, 2 * third, 3 * LANES, LANES), (2 * third, third, 3 * LANES, LANES), (0, length, LANES, LANES)]
        parts = [Part(box, bits) for box in boxes[:4]] + [Part(boxes[4], far)]
        steps = [(0, -1), (4, -1), (1, -1), (2, -1), (0, 0), (3, -1), (4, 0), (1, 0), (0, 1), (4, 1), (2, 0), (1, 1), (3, 0), (2, 1), (3, 1), (0, 2), (1, 2), (2, 2), (4, 2), (3, 2)]
    else:
        parts = [Part((0, length, LANES * at, LANES), far if at == 1 else bits) for at in range(count)]
        steps = [(at, wave - at - 1) for wave in range(count + len(bits)) for at in range(count) if -1 <= wave - at - 1 < len(bits)]
    return parts, steps


def across(x, bit):
    count = lax.axis_size("tp")
    return lax.ppermute(x, "tp", [(i, i ^ (1 << bit)) for i in range(count)])


def after(x, axis):
    count = lax.axis_size(axis)
    return lax.ppermute(x, axis, [(i, (i + 1) % count) for i in range(count)])


def later_rounds(message, inner_end, streams, taps, decay, init_state):
    first = lax.axis_index("ctx") == 0
    poles = decay.shape[0]
    tap_count = taps.shape[1]
    lag = tap_count - 1
    length = streams.shape[2]
    rims = message[poles:].reshape(3, PAD, -1)
    joined = jnp.concatenate([rims, streams[:, 0, :PAD].astype(F32)], axis=1)
    featured = sum(taps[:, i][:, None, :] * joined[:, PAD - i : 2 * PAD - i, :] for i in range(tap_count))
    head = jnp.where(first, 0.0, featured[1] * featured[2])
    local = jnp.where(first, 0.0, inner_end)

    def one(_, incoming):
        state = jnp.where(first, init_state[0], incoming)
        for j in range(lag):
            state = decay * state + head[j][None]
        ended = jnp.where(first, inner_end, local + power(decay, length - lag) * state)
        return after(ended, "ctx")

    state = lax.fori_loop(0, lax.axis_size("ctx") - 2, one, message[:poles])
    return jnp.concatenate([state, message[poles:]], axis=0)


def per_device(streams, taps, decay, residues, init_state, out_weight):
    length, channels = streams.shape[2:]
    poles = decay.shape[0]
    tiles = channels // LANES
    seg_len, turn = segments(length)
    peers = lax.axis_size("tp")
    width = out_weight.shape[1] // peers
    me = lax.axis_index("tp")
    where = jnp.stack([lax.axis_index("ctx"), me & 1, me >> 1]).astype(jnp.int32)
    rows = poles + 3 * PAD
    streams_hbm, weight_hbm = in_hbm(streams), in_hbm(out_weight)
    split = (tiles, seg_len, SEGS, LANES)
    columns = jax.ShapeDtypeStruct((peers // 2, channels, width), BF16)
    driven, inner, message, sent = pl.pallas_call(
        driven_kernel,
        out_shape=(
            jax.ShapeDtypeStruct(split, F32),
            jax.ShapeDtypeStruct((tiles, poles, SEGS, LANES), F32),
            jax.ShapeDtypeStruct((rows, channels), F32),
            columns,
        ),
        in_specs=[SMEM, HBM, HBM, HBM, HBM, HBM],
        out_specs=(VMEM, VMEM, VMEM, VMEM),
        scratch_shapes=[
            pltpu.VMEM((2, EDGE + length, LANES), F32),
            pltpu.VMEM((tiles, 2, length, LANES), BF16),
            pltpu.VMEM((3, 16, channels), BF16),
            pltpu.VMEM(taps.shape, F32),
            pltpu.VMEM(decay.shape, F32),
            pltpu.VMEM(init_state.shape, F32),
            pltpu.SemaphoreType.DMA((peers // 2,)),
            pltpu.SemaphoreType.DMA((4 + tiles,)),
        ],
        compiler_params=pltpu.CompilerParams(vmem_limit_bytes=LIMIT),
        cost_estimate=QUICK,
        name="driven",
    )(where, streams_hbm, in_hbm(taps), in_hbm(decay), in_hbm(init_state), weight_hbm)
    passed = after(message, "ctx")
    theirs = across(sent, 0)
    response, query, mine = pl.pallas_call(
        response_kernel,
        out_shape=(
            jax.ShapeDtypeStruct(split, F32),
            jax.ShapeDtypeStruct(split, F32),
            columns,
        ),
        in_specs=[SMEM] + [VMEM] * 6 + [HBM],
        out_specs=(VMEM, VMEM, VMEM),
        scratch_shapes=[pltpu.VMEM((EDGE + length, LANES), F32), pltpu.SemaphoreType.DMA((peers // 2,))],
        compiler_params=pltpu.CompilerParams(vmem_limit_bytes=LIMIT),
        cost_estimate=QUICK,
        name="response",
    )(where, streams, taps, decay, residues, driven, inner, weight_hbm)
    if lax.axis_size("ctx") > 2:
        passed = later_rounds(passed, message[:poles], streams, taps, decay, init_state)
    gated = pl.pallas_call(
        gated_kernel,
        out_shape=jax.ShapeDtypeStruct((length, channels), BF16),
        in_specs=[SMEM] + [VMEM] * 8,
        out_specs=VMEM,
        scratch_shapes=[
            pltpu.VMEM((PAD + 16, channels), F32),
            pltpu.VMEM((2 * poles, channels), F32),
            pltpu.VMEM((PAD + length, LANES), F32),
            pltpu.VMEM((PAD, channels), F32),
        ],
        compiler_params=pltpu.CompilerParams(vmem_limit_bytes=LIMIT),
        cost_estimate=QUICK,
        name="gated",
    )(where, passed, streams, taps, decay, residues, init_state, response, query)
    other = across(gated, 0)

    parts, steps = plan(peers, length, width)
    flying, kept, finished, ordered = {}, {}, {}, gated
    started = project_own(parts[steps[0][0]], where, gated, mine)
    for at, stage in steps:
        part = parts[at]
        if stage < 0:
            if at == steps[0][0]:
                send, kept[at] = project_other(part, where, started, other, theirs)
            else:
                send, kept[at] = project(part, where, gated, other, mine, theirs, ordered)
            ordered = send
        elif stage + 1 < len(part.order):
            send, kept[at] = merge(kept[at], flying[at], ordered)
            ordered = send
        elif len(finished) + 1 < len(parts):
            ordered = finished[at] = finish(kept[at], flying[at], ordered)
            continue
        else:
            boxes = [parts[done].box for done in finished] + [part.box]
            return gather(list(finished.values()), boxes, kept[at], flying[at], ordered, length, width)
        flying[at] = across(send, part.order[stage + 1])


def solution(mesh):
    in_specs = (
        P(None, None, "ctx", "tp"),
        P(None, None, "tp"),
        P(None, "tp"),
        P(None, "tp"),
        P(None, None, "tp"),
        P("tp", None),
    )
    out_specs = P(None, "ctx", "tp")
    return jax.shard_map(
        per_device, mesh=mesh, in_specs=in_specs, out_specs=out_specs, check_vma=False
    )
```

```python
import dataclasses
import functools

import jax
import jax.numpy as jnp
from jax import lax
from jax.experimental import pallas as pl
from jax.experimental.pallas import tpu as pltpu
from jax.sharding import PartitionSpec as P

F32 = jnp.float32
BF16 = jnp.bfloat16
LANES = 128
SEGS = 8
PAD = 8
EDGE = 2 * PAD


def power(base, exponent):
    result, square = None, base
    while exponent:
        if exponent & 1:
            result = square if result is None else result * square
        exponent >>= 1
        if exponent:
            square = square * square
    return result


def segments(length):
    seg_len = (length + PAD) // SEGS
    return seg_len, next(n for n in (7, 8, 6, 5, 4, 3, 2, 1) if seg_len % n == 0)


def tree_sum(terms):
    while len(terms) > 1:
        paired = [a + b for a, b in zip(terms[::2], terms[1::2])]
        terms = paired + terms[len(paired) * 2 :]
    return terms[0]


def weight_columns(weight_hbm, ref, side, sems):
    parts, _, width = ref.shape
    copies = []
    for part in range(parts):
        column = pl.multiple_of((2 * part + side) * width, LANES)
        copies.append(pltpu.make_async_copy(weight_hbm.at[:, pl.ds(column, width)], ref.at[part], sems.at[part]))
    return copies


def driven_kernel(where_ref, streams_hbm, taps_hbm, decay_hbm, init_hbm, weight_hbm, driven_ref, inner_ref, message_ref, sent_ref, wide_ref, streams_ref, rim_ref, taps_ref, decay_ref, init_ref, weight_sems, sems):
    first = where_ref[0] == 0
    core = where_ref[1]
    poles = decay_ref.shape[0]
    tap_count = taps_ref.shape[1]
    length, channels = streams_hbm.shape[2:]
    tiles = channels // LANES
    seg_len, turn = segments(length)
    small = [
        pltpu.make_async_copy(taps_hbm, taps_ref, sems.at[0]),
        pltpu.make_async_copy(decay_hbm, decay_ref, sems.at[1]),
        pltpu.make_async_copy(init_hbm, init_ref, sems.at[2]),
        pltpu.make_async_copy(streams_hbm.at[:, 0, length - 16 :], rim_ref, sems.at[3]),
    ]
    loads = []
    for tile in range(tiles):
        lanes = pl.ds(tile * LANES, LANES)
        loads.append(pltpu.make_async_copy(streams_hbm.at[1:3, 0, :, lanes], streams_ref.at[tile], sems.at[4 + tile]))
    loads[0].start()
    for copy in small + loads[1:]:
        copy.start()
    copies = weight_columns(weight_hbm, sent_ref, 1 - core, weight_sems)
    for copy in small:
        copy.wait()
    sublane = lax.broadcasted_iota(jnp.int32, (SEGS, LANES), 0)
    for tile in range(tiles):
        lanes = slice(tile * LANES, (tile + 1) * LANES)
        loads[tile].wait()
        if tile < 2:
            for copy in copies[tile::2]:
                copy.start()
        for s in range(2):
            wide_ref[s, 0:EDGE, :] = jnp.zeros((EDGE, LANES), F32)
            wide_ref[s, EDGE : EDGE + length, :] = streams_ref[tile, s].astype(F32)
        taps = [[jnp.broadcast_to(taps_ref[1 + s, i : i + 1, lanes], (SEGS, LANES)) for i in range(tap_count)] for s in range(2)]

        def row(s, j):
            return wide_ref[s, pl.ds(PAD + j, SEGS, stride=seg_len), :]

        def block(base, windows):
            windows = list(windows)
            for step in range(turn):
                made = []
                for s in range(2):
                    seen = list(windows[s]) + [row(s, base + step)]
                    made.append(tree_sum([taps[s][i] * seen[-1 - i] for i in range(tap_count)]))
                    windows[s] = tuple(seen[1:])
                driven_ref[tile, base + step] = made[0] * made[1]
            return tuple(windows)

        windows = tuple(tuple(row(s, j - (tap_count - 1)) for j in range(tap_count - 1)) for s in range(2))
        lax.fori_loop(0, seg_len // turn, lambda b, w: block(b * turn, w), windows)
        for j in range(tap_count - 1):
            driven_ref[tile, PAD + j, 0:1, :] = jnp.where(first, driven_ref[tile, PAD + j, 0:1, :], 0.0)

        decays = [jnp.broadcast_to(decay_ref[n : n + 1, lanes], (SEGS, LANES)) for n in range(poles)]

        def scan(b, states):
            states = list(states)
            for step in range(turn):
                value = driven_ref[tile, b * turn + step]
                states = [d * s + value for d, s in zip(decays, states)]
            return tuple(states)

        zero = jnp.zeros((SEGS, LANES), F32)
        ends = lax.fori_loop(0, seg_len // turn, scan, (zero,) * poles)
        for n in range(poles):
            total, factor = ends[n], power(decays[n], seg_len)
            for reach in (1, 2, 4):
                moved = jnp.where(sublane >= reach, pltpu.roll(total, reach, 0), 0.0)
                total = total + factor * moved
                factor = factor * factor
            inner_ref[tile, n] = total
            message_ref[n : n + 1, lanes] = total[SEGS - 1 : SEGS, :]
    carried = power(decay_ref[...], length) * init_ref[0]
    message_ref[0:poles, :] = message_ref[0:poles, :] + jnp.where(first, carried, 0.0)
    for s in range(3):
        message_ref[poles + s * PAD : poles + (s + 1) * PAD, :] = rim_ref[s].astype(F32)[16 - PAD :]
    for copy in copies:
        copy.wait()


def response_kernel(where_ref, query_in_ref, taps_ref, decay_ref, residues_ref, driven_ref, inner_ref, weight_hbm, response_ref, query_ref, mine_ref, wide_ref, weight_sems):
    poles = decay_ref.shape[0]
    tap_count = taps_ref.shape[1]
    lag = tap_count - 1
    length, channels = query_in_ref.shape[2:]
    tiles = channels // LANES
    seg_len, turn = segments(length)
    copies = weight_columns(weight_hbm, mine_ref, where_ref[1], weight_sems)
    for copy in copies:
        copy.start()
    sublane = lax.broadcasted_iota(jnp.int32, (SEGS, LANES), 0)
    for tile in range(tiles):
        lanes = slice(tile * LANES, (tile + 1) * LANES)
        wide_ref[0:EDGE, :] = jnp.zeros((EDGE, LANES), F32)
        wide_ref[EDGE : EDGE + length, :] = query_in_ref[0, 0, :, lanes].astype(F32)
        taps = [jnp.broadcast_to(taps_ref[0, i : i + 1, lanes], (SEGS, LANES)) for i in range(tap_count)]

        def row(j):
            return wide_ref[pl.ds(PAD + j, SEGS, stride=seg_len), :]

        def fir(b, window):
            window = list(window)
            for step in range(turn):
                window.append(row(b * turn + step))
                query_ref[tile, b * turn + step] = tree_sum([taps[i] * window[-1 - i] for i in range(tap_count)])
                window = window[1:]
            return tuple(window)

        lax.fori_loop(0, seg_len // turn, fir, tuple(row(j - lag) for j in range(lag)))

        decays = [jnp.broadcast_to(decay_ref[n : n + 1, lanes], (SEGS, LANES)) for n in range(poles)]
        weights = [jnp.broadcast_to(residues_ref[n : n + 1, lanes], (SEGS, LANES)) for n in range(poles)]
        states = [jnp.where(sublane == 0, 0.0, pltpu.roll(inner_ref[tile, n], 1, 0)) for n in range(poles)]

        def scan(b, states):
            states = list(states)
            for step in range(turn):
                value = driven_ref[tile, b * turn + step]
                states = [d * s + value for d, s in zip(decays, states)]
                response_ref[tile, b * turn + step] = tree_sum([r * s for r, s in zip(weights, states)])
            return tuple(states)

        lax.fori_loop(0, seg_len // turn, scan, tuple(states))
    for copy in copies:
        copy.wait()


def gated_kernel(where_ref, message_ref, head_in_ref, taps_ref, decay_ref, residues_ref, init_ref, response_ref, query_ref, gated_ref, head_ref, start_ref, out_ref, early_ref):
    first = where_ref[0] == 0
    poles = decay_ref.shape[0]
    tap_count = taps_ref.shape[1]
    lag = tap_count - 1
    length, channels = gated_ref.shape
    tiles = channels // LANES
    seg_len, turn = segments(length)
    sublane = lax.broadcasted_iota(jnp.int32, (SEGS, LANES), 0)

    heads = []
    for s in range(3):
        head_ref[0:PAD, :] = jnp.where(first, 0.0, message_ref[poles + s * PAD : poles + (s + 1) * PAD, :])
        head_ref[PAD : PAD + 16, :] = head_in_ref[s, 0, 0:16, :].astype(F32)
        heads.append(tree_sum([taps_ref[s, i : i + 1, :] * head_ref[PAD - i : 2 * PAD - i, :] for i in range(tap_count)]))
    head_query = heads[0]
    counted = jnp.where(first, 0.0, heads[1] * heads[2])
    decay, residues = decay_ref[...], residues_ref[...]
    state = jnp.where(first, init_ref[0], message_ref[0:poles, :])
    for j in range(lag):
        state = decay * state + counted[j : j + 1, :]
        early_ref[j : j + 1, :] = jnp.sum(residues * state, axis=0, keepdims=True)
    state = state * residues
    start_ref[0:poles, :] = state / power(decay, PAD + lag)
    start_ref[poles:, :] = state * power(decay, seg_len - PAD - lag)

    for tile in range(tiles):
        lanes = slice(tile * LANES, (tile + 1) * LANES)
        decays = [jnp.broadcast_to(decay_ref[n : n + 1, lanes], (SEGS, LANES)) for n in range(poles)]
        states = []
        for n in range(poles):
            factor = power(decays[n], seg_len)
            spread = jnp.broadcast_to(start_ref[poles + n : poles + n + 1, lanes], (SEGS, LANES))
            before = sublane - 1
            for bit in (1, 2, 4):
                spread = jnp.where(jnp.bitwise_and(before, bit) != 0, spread * factor, spread)
                factor = factor * factor
            own = jnp.broadcast_to(start_ref[n : n + 1, lanes], (SEGS, LANES))
            states.append(jnp.where(sublane == 0, own, spread))

        def block(b, states):
            states = list(states)
            for step in range(turn):
                at = b * turn + step
                states = [d * s for d, s in zip(decays, states)]
                total = response_ref[tile, at] + tree_sum(states)
                out_ref[pl.ds(at, SEGS, stride=seg_len), :] = total * query_ref[tile, at]
            return tuple(states)

        lax.fori_loop(0, seg_len // turn, block, tuple(states))
        for j in range(lag):
            total = response_ref[tile, PAD + j, 0:1, :] + early_ref[j : j + 1, lanes]
            out_ref[PAD + j : PAD + j + 1, :] = total * head_query[j : j + 1, lanes]
        gated_ref[:, lanes] = out_ref[PAD:, :].astype(BF16)


def relative(index, high, order):
    value = high << (order[0] - 1)
    count = len(order) - 1
    for place, bit in enumerate(order[1:]):
        value = value | (((index >> (count - 1 - place)) & 1) << (bit - 1))
    return value


def sides(part, where_ref, weight_ref, index):
    _, _, column, columns = part.box
    blocks = [relative(index, high, part.order) ^ where_ref[2] for high in (1, 0)]
    return jnp.concatenate([weight_ref[block, :, column : column + columns] for block in blocks], axis=1)


def project_kernel(part, where_ref, own_ref, other_ref, mine_ref, theirs_ref, order_ref, send_ref, keep_ref):
    row, rows, _, columns = part.box
    wide = jnp.concatenate([own_ref[row : row + rows, :], other_ref[row : row + rows, :]], axis=1)

    def step(index):
        both = jnp.concatenate([sides(part, where_ref, ref, index) for ref in (mine_ref, theirs_ref)], axis=0)
        total = jnp.dot(wide, both, preferred_element_type=F32)
        send_ref[index] = total[:, :columns].astype(BF16)
        keep_ref[index] = total[:, columns:]

    for index in range(send_ref.shape[0]):
        step(index)


def project_own_kernel(part, where_ref, own_ref, mine_ref, out_ref):
    row, rows, _, _ = part.box

    def step(index):
        out_ref[index] = jnp.dot(own_ref[row : row + rows, :], sides(part, where_ref, mine_ref, index), preferred_element_type=F32)

    for index in range(out_ref.shape[0]):
        step(index)


def project_other_kernel(part, where_ref, sum_ref, other_ref, theirs_ref, send_ref, keep_ref):
    row, rows, _, columns = part.box

    def step(index):
        total = sum_ref[index] + jnp.dot(other_ref[row : row + rows, :], sides(part, where_ref, theirs_ref, index), preferred_element_type=F32)
        send_ref[index] = total[:, :columns].astype(BF16)
        keep_ref[index] = total[:, columns:]

    for index in range(send_ref.shape[0]):
        step(index)


def merge_kernel(keep_ref, received_ref, order_ref, send_ref, kept_ref):
    half = kept_ref.shape[0]
    send_ref[...] = (keep_ref[half:] + received_ref[half:].astype(F32)).astype(BF16)
    kept_ref[...] = keep_ref[:half] + received_ref[:half].astype(F32)


def finish_kernel(keep_ref, received_ref, order_ref, out_ref):
    out_ref[...] = (keep_ref[0] + received_ref[0].astype(F32)).astype(BF16)


def gather_kernel(boxes, *refs):
    count = len(boxes) - 1
    pieces, (keep_ref, received_ref, order_ref, out_ref, last_ref, sems) = refs[:count], refs[count:]
    copies = []
    for at, (piece, (row, rows, column, columns)) in enumerate(zip(list(pieces) + [last_ref], boxes)):
        if at == count:
            last_ref[...] = (keep_ref[0] + received_ref[0].astype(F32)).astype(BF16)
        place = out_ref.at[0, pl.ds(row, rows), pl.ds(column, columns)]
        copies.append(pltpu.make_async_copy(piece, place, sems.at[at]))
        copies[-1].start()
    for copy in copies:
        copy.wait()


SMEM = pl.BlockSpec(memory_space=pltpu.SMEM)
VMEM = pl.BlockSpec(memory_space=pltpu.VMEM)
HBM = pl.BlockSpec(memory_space=pltpu.HBM)
ANYWHERE = pl.BlockSpec(memory_space=pl.ANY)
LIMIT = 24 * 1024 * 1024
QUICK = pl.CostEstimate(flops=1, bytes_accessed=1, transcendentals=0)


def in_hbm(x):
    return pltpu.with_memory_space_constraint(x, pltpu.MemorySpace.HBM)


@dataclasses.dataclass(frozen=True)
class Part:
    box: tuple
    order: tuple


def project(part, where, own, other, mine, theirs, ordered):
    channels = own.shape[1]
    halves = mine.shape[0]
    rest = halves // 2
    _, rows, _, columns = part.box
    return pl.pallas_call(
        functools.partial(project_kernel, part),
        out_shape=(jax.ShapeDtypeStruct((rest, rows, columns), BF16), jax.ShapeDtypeStruct((rest, rows, columns), F32)),
        in_specs=[SMEM, VMEM, VMEM, VMEM, VMEM, ANYWHERE],
        out_specs=(VMEM, VMEM),
        compiler_params=pltpu.CompilerParams(vmem_limit_bytes=LIMIT),
        cost_estimate=QUICK,
        name="project",
    )(where, own, other, mine, theirs, ordered)


def project_own(part, where, own, mine):
    _, rows, _, columns = part.box
    return pl.pallas_call(
        functools.partial(project_own_kernel, part),
        out_shape=jax.ShapeDtypeStruct((mine.shape[0] // 2, rows, 2 * columns), F32),
        in_specs=[SMEM, VMEM, VMEM],
        out_specs=VMEM,
        compiler_params=pltpu.CompilerParams(vmem_limit_bytes=LIMIT),
        cost_estimate=QUICK,
        name="project_own",
    )(where, own, mine)


def project_other(part, where, total, other, theirs):
    _, rows, _, columns = part.box
    shape = (total.shape[0], rows, columns)
    return pl.pallas_call(
        functools.partial(project_other_kernel, part),
        out_shape=(jax.ShapeDtypeStruct(shape, BF16), jax.ShapeDtypeStruct(shape, F32)),
        in_specs=[SMEM, VMEM, VMEM, VMEM],
        out_specs=(VMEM, VMEM),
        compiler_params=pltpu.CompilerParams(vmem_limit_bytes=LIMIT),
        cost_estimate=QUICK,
        name="project_other",
    )(where, total, other, theirs)


def merge(keep, received, ordered):
    half = keep.shape[0] // 2
    shape = (half,) + keep.shape[1:]
    return pl.pallas_call(
        merge_kernel,
        out_shape=(jax.ShapeDtypeStruct(shape, BF16), jax.ShapeDtypeStruct(shape, F32)),
        in_specs=[VMEM, VMEM, ANYWHERE],
        out_specs=(VMEM, VMEM),
        compiler_params=pltpu.CompilerParams(vmem_limit_bytes=LIMIT),
        cost_estimate=QUICK,
        name="merge",
    )(keep, received, ordered)


def finish(keep, received, ordered):
    return pl.pallas_call(
        finish_kernel,
        out_shape=jax.ShapeDtypeStruct(keep.shape[1:], BF16),
        in_specs=[VMEM, VMEM, ANYWHERE],
        out_specs=VMEM,
        compiler_params=pltpu.CompilerParams(vmem_limit_bytes=LIMIT),
        cost_estimate=QUICK,
        name="finish",
    )(keep, received, ordered)


def gather(pieces, boxes, keep, received, ordered, length, width):
    return pl.pallas_call(
        functools.partial(gather_kernel, boxes),
        out_shape=jax.ShapeDtypeStruct((1, length, width), BF16),
        in_specs=[VMEM] * len(pieces) + [VMEM, VMEM, ANYWHERE],
        out_specs=HBM,
        scratch_shapes=[pltpu.VMEM(keep.shape[1:], BF16), pltpu.SemaphoreType.DMA((len(boxes),))],
        compiler_params=pltpu.CompilerParams(vmem_limit_bytes=LIMIT),
        cost_estimate=QUICK,
        name="gather",
    )(*pieces, keep, received, ordered)


def plan(peers, length, width):
    bits = tuple(range(1, peers.bit_length() - 1))
    far = bits[-2:] + bits[:-2]
    count = width // LANES
    if count == 4 and len(bits) == 3 and length % 48 == 0:
        third = length // 3
        boxes = [(0, length, 0, LANES), (0, length, 2 * LANES, LANES), (0, 2 * third, 3 * LANES, LANES), (2 * third, third, 3 * LANES, LANES), (0, length, LANES, LANES)]
        parts = [Part(box, bits) for box in boxes[:4]] + [Part(boxes[4], far)]
        steps = [(0, -1), (4, -1), (1, -1), (2, -1), (3, -1), (0, 0), (4, 0), (1, 0), (0, 1), (4, 1), (2, 0), (1, 1), (3, 0), (2, 1), (3, 1), (0, 2), (1, 2), (2, 2), (4, 2), (3, 2)]
    else:
        parts = [Part((0, length, LANES * at, LANES), far if at == 1 else bits) for at in range(count)]
        steps = [(at, wave - at - 1) for wave in range(count + len(bits)) for at in range(count) if -1 <= wave - at - 1 < len(bits)]
    return parts, steps


def across(x, bit):
    count = lax.axis_size("tp")
    return lax.ppermute(x, "tp", [(i, i ^ (1 << bit)) for i in range(count)])


def after(x, axis):
    count = lax.axis_size(axis)
    return lax.ppermute(x, axis, [(i, (i + 1) % count) for i in range(count)])


def later_rounds(message, inner_end, streams, taps, decay, init_state):
    first = lax.axis_index("ctx") == 0
    poles = decay.shape[0]
    tap_count = taps.shape[1]
    lag = tap_count - 1
    length = streams.shape[2]
    rims = message[poles:].reshape(3, PAD, -1)
    joined = jnp.concatenate([rims, streams[:, 0, :PAD].astype(F32)], axis=1)
    featured = sum(taps[:, i][:, None, :] * joined[:, PAD - i : 2 * PAD - i, :] for i in range(tap_count))
    head = jnp.where(first, 0.0, featured[1] * featured[2])
    local = jnp.where(first, 0.0, inner_end)

    def one(_, incoming):
        state = jnp.where(first, init_state[0], incoming)
        for j in range(lag):
            state = decay * state + head[j][None]
        ended = jnp.where(first, inner_end, local + power(decay, length - lag) * state)
        return after(ended, "ctx")

    state = lax.fori_loop(0, lax.axis_size("ctx") - 2, one, message[:poles])
    return jnp.concatenate([state, message[poles:]], axis=0)


def per_device(streams, taps, decay, residues, init_state, out_weight):
    length, channels = streams.shape[2:]
    poles = decay.shape[0]
    tiles = channels // LANES
    seg_len, turn = segments(length)
    peers = lax.axis_size("tp")
    width = out_weight.shape[1] // peers
    me = lax.axis_index("tp")
    where = jnp.stack([lax.axis_index("ctx"), me & 1, me >> 1]).astype(jnp.int32)
    rows = poles + 3 * PAD
    streams_hbm, weight_hbm = in_hbm(streams), in_hbm(out_weight)
    split = (tiles, seg_len, SEGS, LANES)
    columns = jax.ShapeDtypeStruct((peers // 2, channels, width), BF16)
    driven, inner, message, sent = pl.pallas_call(
        driven_kernel,
        out_shape=(
            jax.ShapeDtypeStruct(split, F32),
            jax.ShapeDtypeStruct((tiles, poles, SEGS, LANES), F32),
            jax.ShapeDtypeStruct((rows, channels), F32),
            columns,
        ),
        in_specs=[SMEM, HBM, HBM, HBM, HBM, HBM],
        out_specs=(VMEM, VMEM, VMEM, VMEM),
        scratch_shapes=[
            pltpu.VMEM((2, EDGE + length, LANES), F32),
            pltpu.VMEM((tiles, 2, length, LANES), BF16),
            pltpu.VMEM((3, 16, channels), BF16),
            pltpu.VMEM(taps.shape, F32),
            pltpu.VMEM(decay.shape, F32),
            pltpu.VMEM(init_state.shape, F32),
            pltpu.SemaphoreType.DMA((peers // 2,)),
            pltpu.SemaphoreType.DMA((4 + tiles,)),
        ],
        compiler_params=pltpu.CompilerParams(vmem_limit_bytes=LIMIT),
        cost_estimate=QUICK,
        name="driven",
    )(where, streams_hbm, in_hbm(taps), in_hbm(decay), in_hbm(init_state), weight_hbm)
    passed = after(message, "ctx")
    theirs = across(sent, 0)
    response, query, mine = pl.pallas_call(
        response_kernel,
        out_shape=(
            jax.ShapeDtypeStruct(split, F32),
            jax.ShapeDtypeStruct(split, F32),
            columns,
        ),
        in_specs=[SMEM] + [VMEM] * 6 + [HBM],
        out_specs=(VMEM, VMEM, VMEM),
        scratch_shapes=[pltpu.VMEM((EDGE + length, LANES), F32), pltpu.SemaphoreType.DMA((peers // 2,))],
        compiler_params=pltpu.CompilerParams(vmem_limit_bytes=LIMIT),
        cost_estimate=QUICK,
        name="response",
    )(where, streams, taps, decay, residues, driven, inner, weight_hbm)
    if lax.axis_size("ctx") > 2:
        passed = later_rounds(passed, message[:poles], streams, taps, decay, init_state)
    gated = pl.pallas_call(
        gated_kernel,
        out_shape=jax.ShapeDtypeStruct((length, channels), BF16),
        in_specs=[SMEM] + [VMEM] * 8,
        out_specs=VMEM,
        scratch_shapes=[
            pltpu.VMEM((PAD + 16, channels), F32),
            pltpu.VMEM((2 * poles, channels), F32),
            pltpu.VMEM((PAD + length, LANES), F32),
            pltpu.VMEM((PAD, channels), F32),
        ],
        compiler_params=pltpu.CompilerParams(vmem_limit_bytes=LIMIT),
        cost_estimate=QUICK,
        name="gated",
    )(where, passed, streams, taps, decay, residues, init_state, response, query)
    other = across(gated, 0)

    parts, steps = plan(peers, length, width)
    flying, kept, finished, ordered = {}, {}, {}, gated
    started = project_own(parts[steps[0][0]], where, gated, mine)
    for at, stage in steps:
        part = parts[at]
        if stage < 0:
            if at == steps[0][0]:
                send, kept[at] = project_other(part, where, started, other, theirs)
            else:
                send, kept[at] = project(part, where, gated, other, mine, theirs, ordered)
            ordered = send
        elif stage + 1 < len(part.order):
            send, kept[at] = merge(kept[at], flying[at], ordered)
            ordered = send
        elif len(finished) + 1 < len(parts):
            ordered = finished[at] = finish(kept[at], flying[at], ordered)
            continue
        else:
            boxes = [parts[done].box for done in finished] + [part.box]
            return gather(list(finished.values()), boxes, kept[at], flying[at], ordered, length, width)
        flying[at] = across(send, part.order[stage + 1])


def solution(mesh):
    in_specs = (
        P(None, None, "ctx", "tp"),
        P(None, None, "tp"),
        P(None, "tp"),
        P(None, "tp"),
        P(None, None, "tp"),
        P("tp", None),
    )
    out_specs = P(None, "ctx", "tp")
    return jax.shard_map(
        per_device, mesh=mesh, in_specs=in_specs, out_specs=out_specs, check_vma=False
    )
```

```python
import dataclasses
import functools

import jax
import jax.numpy as jnp
from jax import lax
from jax.experimental import pallas as pl
from jax.experimental.pallas import tpu as pltpu
from jax.sharding import PartitionSpec as P

F32 = jnp.float32
BF16 = jnp.bfloat16
LANES = 128
SEGS = 8
PAD = 8
EDGE = 2 * PAD
SPARE = 64


def power(base, exponent):
    result, square = None, base
    while exponent:
        if exponent & 1:
            result = square if result is None else result * square
        exponent >>= 1
        if exponent:
            square = square * square
    return result


def segments(length):
    seg_len = (length + PAD) // SEGS
    return seg_len, next(n for n in (7, 8, 6, 5, 4, 3, 2, 1) if seg_len % n == 0)


def tree_sum(terms):
    while len(terms) > 1:
        paired = [a + b for a, b in zip(terms[::2], terms[1::2])]
        terms = paired + terms[len(paired) * 2 :]
    return terms[0]


def weight_columns(weight_hbm, ref, side, sems):
    parts, _, width = ref.shape
    copies = []
    for part in range(parts):
        column = pl.multiple_of((2 * part + side) * width, LANES)
        copies.append(pltpu.make_async_copy(weight_hbm.at[:, pl.ds(column, width)], ref.at[part], sems.at[part]))
    return copies


def driven_kernel(where_ref, streams_hbm, taps_hbm, decay_hbm, init_hbm, weight_hbm, driven_ref, inner_ref, message_ref, sent_ref, wide_ref, streams_ref, rim_ref, taps_ref, decay_ref, init_ref, weight_sems, sems):
    first = where_ref[0] == 0
    core = where_ref[1]
    poles = decay_ref.shape[0]
    tap_count = taps_ref.shape[1]
    length, channels = streams_hbm.shape[2:]
    tiles = channels // LANES
    seg_len, turn = segments(length)
    small = [
        pltpu.make_async_copy(taps_hbm, taps_ref, sems.at[0]),
        pltpu.make_async_copy(decay_hbm, decay_ref, sems.at[1]),
        pltpu.make_async_copy(init_hbm, init_ref, sems.at[2]),
        pltpu.make_async_copy(streams_hbm.at[:, 0, length - 16 :], rim_ref, sems.at[3]),
    ]
    loads = []
    for tile in range(tiles):
        lanes = pl.ds(tile * LANES, LANES)
        loads.append(pltpu.make_async_copy(streams_hbm.at[1:3, 0, :, lanes], streams_ref.at[tile], sems.at[4 + tile]))
    loads[0].start()
    for copy in small[:2] + loads[1:] + small[2:]:
        copy.start()
    copies = weight_columns(weight_hbm, sent_ref, 1 - core, weight_sems)
    small[0].wait()
    sublane = lax.broadcasted_iota(jnp.int32, (SEGS, LANES), 0)
    for tile in range(tiles):
        lanes = slice(tile * LANES, (tile + 1) * LANES)
        loads[tile].wait()
        if tile < 2:
            for copy in copies[tile::2]:
                copy.start()
        for s in range(2):
            wide_ref[s, 0:EDGE, :] = jnp.zeros((EDGE, LANES), F32)
            wide_ref[s, EDGE : EDGE + length, :] = streams_ref[tile, s].astype(F32)
        taps = [[jnp.broadcast_to(taps_ref[1 + s, i : i + 1, lanes], (SEGS, LANES)) for i in range(tap_count)] for s in range(2)]

        def row(s, j):
            return wide_ref[s, pl.ds(PAD + j, SEGS, stride=seg_len), :]

        def block(base, windows):
            windows = list(windows)
            for step in range(turn):
                made = []
                for s in range(2):
                    seen = list(windows[s]) + [row(s, base + step)]
                    made.append(tree_sum([taps[s][i] * seen[-1 - i] for i in range(tap_count)]))
                    windows[s] = tuple(seen[1:])
                driven_ref[tile, base + step] = made[0] * made[1]
            return tuple(windows)

        windows = tuple(tuple(row(s, j - (tap_count - 1)) for j in range(tap_count - 1)) for s in range(2))
        lax.fori_loop(0, seg_len // turn, lambda b, w: block(b * turn, w), windows)
        for j in range(tap_count - 1):
            driven_ref[tile, PAD + j, 0:1, :] = jnp.where(first, driven_ref[tile, PAD + j, 0:1, :], 0.0)

        if tile == 0:
            small[1].wait()
        decays = [jnp.broadcast_to(decay_ref[n : n + 1, lanes], (SEGS, LANES)) for n in range(poles)]

        def scan(b, states):
            states = list(states)
            for step in range(turn):
                value = driven_ref[tile, b * turn + step]
                states = [d * s + value for d, s in zip(decays, states)]
            return tuple(states)

        zero = jnp.zeros((SEGS, LANES), F32)
        ends = lax.fori_loop(0, seg_len // turn, scan, (zero,) * poles)
        for n in range(poles):
            total, factor = ends[n], power(decays[n], seg_len)
            for reach in (1, 2, 4):
                moved = jnp.where(sublane >= reach, pltpu.roll(total, reach, 0), 0.0)
                total = total + factor * moved
                factor = factor * factor
            inner_ref[tile, n] = total
            message_ref[n : n + 1, lanes] = total[SEGS - 1 : SEGS, :]
    small[2].wait()
    small[3].wait()
    carried = power(decay_ref[...], length) * init_ref[0]
    message_ref[0:poles, :] = message_ref[0:poles, :] + jnp.where(first, carried, 0.0)
    for s in range(3):
        message_ref[poles + s * PAD : poles + (s + 1) * PAD, :] = rim_ref[s].astype(F32)[16 - PAD :]
    for copy in copies:
        copy.wait()


def response_kernel(where_ref, query_in_ref, taps_ref, decay_ref, residues_ref, driven_ref, inner_ref, weight_hbm, response_ref, query_ref, mine_ref, wide_ref, weight_sems):
    poles = decay_ref.shape[0]
    tap_count = taps_ref.shape[1]
    lag = tap_count - 1
    length, channels = query_in_ref.shape[2:]
    tiles = channels // LANES
    seg_len, turn = segments(length)
    copies = weight_columns(weight_hbm, mine_ref, where_ref[1], weight_sems)
    for copy in copies:
        copy.start()
    sublane = lax.broadcasted_iota(jnp.int32, (SEGS, LANES), 0)
    for tile in range(tiles):
        lanes = slice(tile * LANES, (tile + 1) * LANES)
        wide_ref[0:EDGE, :] = jnp.zeros((EDGE, LANES), F32)
        wide_ref[EDGE : EDGE + length, :] = query_in_ref[0, 0, :, lanes].astype(F32)
        taps = [jnp.broadcast_to(taps_ref[0, i : i + 1, lanes], (SEGS, LANES)) for i in range(tap_count)]

        def row(j):
            return wide_ref[pl.ds(PAD + j, SEGS, stride=seg_len), :]

        def fir(b, window):
            window = list(window)
            for step in range(turn):
                window.append(row(b * turn + step))
                query_ref[tile, b * turn + step] = tree_sum([taps[i] * window[-1 - i] for i in range(tap_count)])
                window = window[1:]
            return tuple(window)

        lax.fori_loop(0, seg_len // turn, fir, tuple(row(j - lag) for j in range(lag)))

        decays = [jnp.broadcast_to(decay_ref[n : n + 1, lanes], (SEGS, LANES)) for n in range(poles)]
        weights = [jnp.broadcast_to(residues_ref[n : n + 1, lanes], (SEGS, LANES)) for n in range(poles)]
        states = [jnp.where(sublane == 0, 0.0, pltpu.roll(inner_ref[tile, n], 1, 0)) for n in range(poles)]

        def scan(b, states):
            states = list(states)
            for step in range(turn):
                value = driven_ref[tile, b * turn + step]
                states = [d * s + value for d, s in zip(decays, states)]
                response_ref[tile, b * turn + step] = tree_sum([r * s for r, s in zip(weights, states)])
            return tuple(states)

        lax.fori_loop(0, seg_len // turn, scan, tuple(states))
    for copy in copies:
        copy.wait()


def gated_kernel(where_ref, message_ref, head_in_ref, taps_ref, decay_ref, residues_ref, init_ref, response_ref, query_ref, gated_ref, head_ref, start_ref, out_ref, early_ref):
    first = where_ref[0] == 0
    poles = decay_ref.shape[0]
    tap_count = taps_ref.shape[1]
    lag = tap_count - 1
    length, channels = gated_ref.shape
    tiles = channels // LANES
    seg_len, turn = segments(length)
    sublane = lax.broadcasted_iota(jnp.int32, (SEGS, LANES), 0)

    heads = []
    for s in range(3):
        head_ref[0:PAD, :] = jnp.where(first, 0.0, message_ref[poles + s * PAD : poles + (s + 1) * PAD, :])
        head_ref[PAD : PAD + 16, :] = head_in_ref[s, 0, 0:16, :].astype(F32)
        heads.append(tree_sum([taps_ref[s, i : i + 1, :] * head_ref[PAD - i : 2 * PAD - i, :] for i in range(tap_count)]))
    head_query = heads[0]
    counted = jnp.where(first, 0.0, heads[1] * heads[2])
    decay, residues = decay_ref[...], residues_ref[...]
    state = jnp.where(first, init_ref[0], message_ref[0:poles, :])
    for j in range(lag):
        state = decay * state + counted[j : j + 1, :]
        early_ref[j : j + 1, :] = jnp.sum(residues * state, axis=0, keepdims=True)
    state = state * residues
    start_ref[0:poles, :] = state / power(decay, PAD + lag)
    start_ref[poles:, :] = state * power(decay, seg_len - PAD - lag)

    for tile in range(tiles):
        lanes = slice(tile * LANES, (tile + 1) * LANES)
        decays = [jnp.broadcast_to(decay_ref[n : n + 1, lanes], (SEGS, LANES)) for n in range(poles)]
        states = []
        for n in range(poles):
            factor = power(decays[n], seg_len)
            spread = jnp.broadcast_to(start_ref[poles + n : poles + n + 1, lanes], (SEGS, LANES))
            before = sublane - 1
            for bit in (1, 2, 4):
                spread = jnp.where(jnp.bitwise_and(before, bit) != 0, spread * factor, spread)
                factor = factor * factor
            own = jnp.broadcast_to(start_ref[n : n + 1, lanes], (SEGS, LANES))
            states.append(jnp.where(sublane == 0, own, spread))

        def block(b, states):
            states = list(states)
            for step in range(turn):
                at = b * turn + step
                states = [d * s for d, s in zip(decays, states)]
                total = response_ref[tile, at] + tree_sum(states)
                out_ref[pl.ds(at, SEGS, stride=seg_len), :] = total * query_ref[tile, at]
            return tuple(states)

        lax.fori_loop(0, seg_len // turn, block, tuple(states))
        for j in range(lag):
            total = response_ref[tile, PAD + j, 0:1, :] + early_ref[j : j + 1, lanes]
            out_ref[PAD + j : PAD + j + 1, :] = total * head_query[j : j + 1, lanes]
        gated_ref[:, lanes] = out_ref[PAD : PAD + length, :].astype(BF16)


def relative(index, high, order):
    value = high << (order[0] - 1)
    count = len(order) - 1
    for place, bit in enumerate(order[1:]):
        value = value | (((index >> (count - 1 - place)) & 1) << (bit - 1))
    return value


def sides(part, where_ref, weight_ref, index):
    _, _, column, columns = part.box
    blocks = [relative(index, high, part.order) ^ where_ref[2] for high in (1, 0)]
    return jnp.concatenate([weight_ref[block, :, column : column + columns] for block in blocks], axis=1)


def project_kernel(part, where_ref, own_ref, other_ref, mine_ref, theirs_ref, order_ref, send_ref, keep_ref):
    row, rows, _, columns = part.box
    wide = jnp.concatenate([own_ref[row : row + rows, :], other_ref[row : row + rows, :]], axis=1)

    def step(index):
        both = jnp.concatenate([sides(part, where_ref, ref, index) for ref in (mine_ref, theirs_ref)], axis=0)
        total = jnp.dot(wide, both, preferred_element_type=F32)
        send_ref[index] = total[:, :columns].astype(BF16)
        keep_ref[index] = total[:, columns:]

    for index in range(send_ref.shape[0]):
        step(index)


def project_own_kernel(part, where_ref, own_ref, mine_ref, out_ref):
    row, rows, _, _ = part.box

    def step(index):
        out_ref[index] = jnp.dot(own_ref[row : row + rows, :], sides(part, where_ref, mine_ref, index), preferred_element_type=F32)

    for index in range(out_ref.shape[0]):
        step(index)


def project_other_kernel(part, where_ref, sum_ref, other_ref, theirs_ref, send_ref, keep_ref):
    row, rows, _, columns = part.box

    def step(index):
        total = sum_ref[index] + jnp.dot(other_ref[row : row + rows, :], sides(part, where_ref, theirs_ref, index), preferred_element_type=F32)
        send_ref[index] = total[:, :columns].astype(BF16)
        keep_ref[index] = total[:, columns:]

    for index in range(send_ref.shape[0]):
        step(index)


def merge_kernel(keep_ref, received_ref, order_ref, send_ref, kept_ref):
    half = kept_ref.shape[0]
    send_ref[...] = (keep_ref[half:] + received_ref[half:].astype(F32)).astype(BF16)
    kept_ref[...] = keep_ref[:half] + received_ref[:half].astype(F32)


def finish_kernel(keep_ref, received_ref, order_ref, out_ref):
    out_ref[...] = (keep_ref[0] + received_ref[0].astype(F32)).astype(BF16)


def gather_kernel(boxes, *refs):
    count = len(boxes) - 1
    pieces, (keep_ref, received_ref, order_ref, out_ref, last_ref, sems) = refs[:count], refs[count:]
    copies = []
    for at, (piece, (row, rows, column, columns)) in enumerate(zip(list(pieces) + [last_ref], boxes)):
        if at == count:
            last_ref[...] = (keep_ref[0] + received_ref[0].astype(F32)).astype(BF16)
        place = out_ref.at[0, pl.ds(row, rows), pl.ds(column, columns)]
        copies.append(pltpu.make_async_copy(piece, place, sems.at[at]))
        copies[-1].start()
    for copy in copies:
        copy.wait()


SMEM = pl.BlockSpec(memory_space=pltpu.SMEM)
VMEM = pl.BlockSpec(memory_space=pltpu.VMEM)
HBM = pl.BlockSpec(memory_space=pltpu.HBM)
ANYWHERE = pl.BlockSpec(memory_space=pl.ANY)
LIMIT = 24 * 1024 * 1024
QUICK = pl.CostEstimate(flops=1, bytes_accessed=1, transcendentals=0)


def in_hbm(x):
    return pltpu.with_memory_space_constraint(x, pltpu.MemorySpace.HBM)


@dataclasses.dataclass(frozen=True)
class Part:
    box: tuple
    order: tuple


def project(part, where, own, other, mine, theirs, ordered):
    channels = own.shape[1]
    halves = mine.shape[0]
    rest = halves // 2
    _, rows, _, columns = part.box
    return pl.pallas_call(
        functools.partial(project_kernel, part),
        out_shape=(jax.ShapeDtypeStruct((rest, rows, columns), BF16), jax.ShapeDtypeStruct((rest, rows, columns), F32)),
        in_specs=[SMEM, VMEM, VMEM, VMEM, VMEM, ANYWHERE],
        out_specs=(VMEM, VMEM),
        compiler_params=pltpu.CompilerParams(vmem_limit_bytes=LIMIT),
        cost_estimate=QUICK,
        name="project",
    )(where, own, other, mine, theirs, ordered)


def project_own(part, where, own, mine):
    _, rows, _, columns = part.box
    return pl.pallas_call(
        functools.partial(project_own_kernel, part),
        out_shape=jax.ShapeDtypeStruct((mine.shape[0] // 2, rows, 2 * columns), F32),
        in_specs=[SMEM, VMEM, VMEM],
        out_specs=VMEM,
        compiler_params=pltpu.CompilerParams(vmem_limit_bytes=LIMIT),
        cost_estimate=QUICK,
        name="project_own",
    )(where, own, mine)


def project_other(part, where, total, other, theirs):
    _, rows, _, columns = part.box
    shape = (total.shape[0], rows, columns)
    return pl.pallas_call(
        functools.partial(project_other_kernel, part),
        out_shape=(jax.ShapeDtypeStruct(shape, BF16), jax.ShapeDtypeStruct(shape, F32)),
        in_specs=[SMEM, VMEM, VMEM, VMEM],
        out_specs=(VMEM, VMEM),
        compiler_params=pltpu.CompilerParams(vmem_limit_bytes=LIMIT),
        cost_estimate=QUICK,
        name="project_other",
    )(where, total, other, theirs)


def merge(keep, received, ordered):
    half = keep.shape[0] // 2
    shape = (half,) + keep.shape[1:]
    return pl.pallas_call(
        merge_kernel,
        out_shape=(jax.ShapeDtypeStruct(shape, BF16), jax.ShapeDtypeStruct(shape, F32)),
        in_specs=[VMEM, VMEM, ANYWHERE],
        out_specs=(VMEM, VMEM),
        compiler_params=pltpu.CompilerParams(vmem_limit_bytes=LIMIT),
        cost_estimate=QUICK,
        name="merge",
    )(keep, received, ordered)


def finish(keep, received, ordered):
    return pl.pallas_call(
        finish_kernel,
        out_shape=jax.ShapeDtypeStruct(keep.shape[1:], BF16),
        in_specs=[VMEM, VMEM, ANYWHERE],
        out_specs=VMEM,
        compiler_params=pltpu.CompilerParams(vmem_limit_bytes=LIMIT),
        cost_estimate=QUICK,
        name="finish",
    )(keep, received, ordered)


def gather(pieces, boxes, keep, received, ordered, length, width):
    return pl.pallas_call(
        functools.partial(gather_kernel, boxes),
        out_shape=jax.ShapeDtypeStruct((1, length, width), BF16),
        in_specs=[VMEM] * len(pieces) + [VMEM, VMEM, ANYWHERE],
        out_specs=HBM,
        scratch_shapes=[pltpu.VMEM(keep.shape[1:], BF16), pltpu.SemaphoreType.DMA((len(boxes),))],
        compiler_params=pltpu.CompilerParams(vmem_limit_bytes=LIMIT),
        cost_estimate=QUICK,
        name="gather",
    )(*pieces, keep, received, ordered)


def plan(peers, length, width):
    bits = tuple(range(1, peers.bit_length() - 1))
    far = bits[-2:] + bits[:-2]
    count = width // LANES
    if count == 4 and len(bits) == 3 and length % 48 == 0:
        third = length // 3
        boxes = [(0, length, 0, LANES), (0, length, 2 * LANES, LANES), (0, 2 * third, 3 * LANES, LANES), (2 * third, third, 3 * LANES, LANES), (0, length, LANES, LANES)]
        parts = [Part(box, bits) for box in boxes[:4]] + [Part(boxes[4], far)]
        steps = [(0, -1), (4, -1), (1, -1), (2, -1), (3, -1), (0, 0), (4, 0), (1, 0), (0, 1), (4, 1), (2, 0), (1, 1), (3, 0), (2, 1), (3, 1), (0, 2), (1, 2), (2, 2), (4, 2), (3, 2)]
    else:
        parts = [Part((0, length, LANES * at, LANES), far if at == 1 else bits) for at in range(count)]
        steps = [(at, wave - at - 1) for wave in range(count + len(bits)) for at in range(count) if -1 <= wave - at - 1 < len(bits)]
    return parts, steps


def across(x, bit):
    count = lax.axis_size("tp")
    return lax.ppermute(x, "tp", [(i, i ^ (1 << bit)) for i in range(count)])


def after(x, axis):
    count = lax.axis_size(axis)
    return lax.ppermute(x, axis, [(i, (i + 1) % count) for i in range(count)])


def later_rounds(message, inner_end, streams, taps, decay, init_state):
    first = lax.axis_index("ctx") == 0
    poles = decay.shape[0]
    tap_count = taps.shape[1]
    lag = tap_count - 1
    length = streams.shape[2]
    rims = message[poles:].reshape(3, PAD, -1)
    joined = jnp.concatenate([rims, streams[:, 0, :PAD].astype(F32)], axis=1)
    featured = sum(taps[:, i][:, None, :] * joined[:, PAD - i : 2 * PAD - i, :] for i in range(tap_count))
    head = jnp.where(first, 0.0, featured[1] * featured[2])
    local = jnp.where(first, 0.0, inner_end)

    def one(_, incoming):
        state = jnp.where(first, init_state[0], incoming)
        for j in range(lag):
            state = decay * state + head[j][None]
        ended = jnp.where(first, inner_end, local + power(decay, length - lag) * state)
        return after(ended, "ctx")

    state = lax.fori_loop(0, lax.axis_size("ctx") - 2, one, message[:poles])
    return jnp.concatenate([state, message[poles:]], axis=0)


def per_device(streams, taps, decay, residues, init_state, out_weight):
    length, channels = streams.shape[2:]
    poles = decay.shape[0]
    tiles = channels // LANES
    seg_len, turn = segments(length)
    peers = lax.axis_size("tp")
    width = out_weight.shape[1] // peers
    me = lax.axis_index("tp")
    where = jnp.stack([lax.axis_index("ctx"), me & 1, me >> 1]).astype(jnp.int32)
    rows = poles + 3 * PAD
    streams_hbm, weight_hbm = in_hbm(streams), in_hbm(out_weight)
    split = (tiles, seg_len, SEGS, LANES)
    columns = jax.ShapeDtypeStruct((peers // 2, channels, width), BF16)
    driven, inner, message, sent = pl.pallas_call(
        driven_kernel,
        out_shape=(
            jax.ShapeDtypeStruct(split, F32),
            jax.ShapeDtypeStruct((tiles, poles, SEGS, LANES), F32),
            jax.ShapeDtypeStruct((rows, channels), F32),
            columns,
        ),
        in_specs=[SMEM, HBM, HBM, HBM, HBM, HBM],
        out_specs=(VMEM, VMEM, VMEM, VMEM),
        scratch_shapes=[
            pltpu.VMEM((2, EDGE + length + SPARE, LANES), F32),
            pltpu.VMEM((tiles, 2, length, LANES), BF16),
            pltpu.VMEM((3, 16, channels), BF16),
            pltpu.VMEM(taps.shape, F32),
            pltpu.VMEM(decay.shape, F32),
            pltpu.VMEM(init_state.shape, F32),
            pltpu.SemaphoreType.DMA((peers // 2,)),
            pltpu.SemaphoreType.DMA((4 + tiles,)),
        ],
        compiler_params=pltpu.CompilerParams(vmem_limit_bytes=LIMIT),
        cost_estimate=QUICK,
        name="driven",
    )(where, streams_hbm, in_hbm(taps), in_hbm(decay), in_hbm(init_state), weight_hbm)
    passed = after(message, "ctx")
    theirs = across(sent, 0)
    response, query, mine = pl.pallas_call(
        response_kernel,
        out_shape=(
            jax.ShapeDtypeStruct(split, F32),
            jax.ShapeDtypeStruct(split, F32),
            columns,
        ),
        in_specs=[SMEM] + [VMEM] * 6 + [HBM],
        out_specs=(VMEM, VMEM, VMEM),
        scratch_shapes=[pltpu.VMEM((EDGE + length + SPARE, LANES), F32), pltpu.SemaphoreType.DMA((peers // 2,))],
        compiler_params=pltpu.CompilerParams(vmem_limit_bytes=LIMIT),
        cost_estimate=QUICK,
        name="response",
    )(where, streams, taps, decay, residues, driven, inner, weight_hbm)
    if lax.axis_size("ctx") > 2:
        passed = later_rounds(passed, message[:poles], streams, taps, decay, init_state)
    gated = pl.pallas_call(
        gated_kernel,
        out_shape=jax.ShapeDtypeStruct((length, channels), BF16),
        in_specs=[SMEM] + [VMEM] * 8,
        out_specs=VMEM,
        scratch_shapes=[
            pltpu.VMEM((PAD + 16, channels), F32),
            pltpu.VMEM((2 * poles, channels), F32),
            pltpu.VMEM((PAD + length + SPARE, LANES), F32),
            pltpu.VMEM((PAD, channels), F32),
        ],
        compiler_params=pltpu.CompilerParams(vmem_limit_bytes=LIMIT),
        cost_estimate=QUICK,
        name="gated",
    )(where, passed, streams, taps, decay, residues, init_state, response, query)
    other = across(gated, 0)

    parts, steps = plan(peers, length, width)
    flying, kept, finished, ordered = {}, {}, {}, gated
    started = project_own(parts[steps[0][0]], where, gated, mine)
    for at, stage in steps:
        part = parts[at]
        if stage < 0:
            if at == steps[0][0]:
                send, kept[at] = project_other(part, where, started, other, theirs)
            else:
                send, kept[at] = project(part, where, gated, other, mine, theirs, ordered)
            ordered = send
        elif stage + 1 < len(part.order):
            send, kept[at] = merge(kept[at], flying[at], ordered)
            ordered = send
        elif len(finished) + 1 < len(parts):
            ordered = finished[at] = finish(kept[at], flying[at], ordered)
            continue
        else:
            boxes = [parts[done].box for done in finished] + [part.box]
            return gather(list(finished.values()), boxes, kept[at], flying[at], ordered, length, width)
        flying[at] = across(send, part.order[stage + 1])


def solution(mesh):
    in_specs = (
        P(None, None, "ctx", "tp"),
        P(None, None, "tp"),
        P(None, "tp"),
        P(None, "tp"),
        P(None, None, "tp"),
        P("tp", None),
    )
    out_specs = P(None, "ctx", "tp")
    return jax.shard_map(
        per_device, mesh=mesh, in_specs=in_specs, out_specs=out_specs, check_vma=False
    )
```

```python
import dataclasses
import functools

import jax
import jax.numpy as jnp
from jax import lax
from jax.experimental import pallas as pl
from jax.experimental.pallas import tpu as pltpu
from jax.sharding import PartitionSpec as P

F32 = jnp.float32
BF16 = jnp.bfloat16
LANES = 128
SEGS = 8
PAD = 8
EDGE = 2 * PAD
SPARE = 64


def power(base, exponent):
    result, square = None, base
    while exponent:
        if exponent & 1:
            result = square if result is None else result * square
        exponent >>= 1
        if exponent:
            square = square * square
    return result


def segments(length):
    seg_len = (length + PAD) // SEGS
    return seg_len, next(n for n in (7, 8, 6, 5, 4, 3, 2, 1) if seg_len % n == 0)


def tree_sum(terms):
    while len(terms) > 1:
        paired = [a + b for a, b in zip(terms[::2], terms[1::2])]
        terms = paired + terms[len(paired) * 2 :]
    return terms[0]


def weight_columns(weight_hbm, ref, side, sems):
    parts, _, width = ref.shape
    copies = []
    for part in range(parts):
        column = pl.multiple_of((2 * part + side) * width, LANES)
        copies.append(pltpu.make_async_copy(weight_hbm.at[:, pl.ds(column, width)], ref.at[part], sems.at[part]))
    return copies


def driven_kernel(where_ref, streams_hbm, taps_hbm, decay_hbm, init_hbm, weight_hbm, driven_ref, inner_ref, message_ref, sent_ref, wide_ref, streams_ref, rim_ref, taps_ref, decay_ref, init_ref, weight_sems, sems):
    first = where_ref[0] == 0
    core = where_ref[1]
    poles = decay_ref.shape[0]
    tap_count = taps_ref.shape[1]
    length, channels = streams_hbm.shape[2:]
    tiles = channels // LANES
    seg_len, turn = segments(length)
    small = [
        pltpu.make_async_copy(taps_hbm, taps_ref, sems.at[0]),
        pltpu.make_async_copy(decay_hbm, decay_ref, sems.at[1]),
        pltpu.make_async_copy(init_hbm, init_ref, sems.at[2]),
        pltpu.make_async_copy(streams_hbm.at[:, 0, length - 16 :], rim_ref, sems.at[3]),
    ]
    loads = []
    for tile in range(tiles):
        lanes = pl.ds(tile * LANES, LANES)
        loads.append(pltpu.make_async_copy(streams_hbm.at[1:3, 0, :, lanes], streams_ref.at[tile], sems.at[4 + tile]))
    loads[0].start()
    for copy in small[:2] + loads[1:] + small[2:]:
        copy.start()
    copies = weight_columns(weight_hbm, sent_ref, 1 - core, weight_sems)
    small[0].wait()
    sublane = lax.broadcasted_iota(jnp.int32, (SEGS, LANES), 0)
    for tile in range(tiles):
        lanes = slice(tile * LANES, (tile + 1) * LANES)
        loads[tile].wait()
        if tile < 2:
            for copy in copies[tile::2]:
                copy.start()
        for s in range(2):
            wide_ref[s, 0:EDGE, :] = jnp.zeros((EDGE, LANES), F32)
            wide_ref[s, EDGE : EDGE + length, :] = streams_ref[tile, s].astype(F32)
        taps = [[jnp.broadcast_to(taps_ref[1 + s, i : i + 1, lanes], (SEGS, LANES)) for i in range(tap_count)] for s in range(2)]

        def row(s, j):
            return wide_ref[s, pl.ds(PAD + j, SEGS, stride=seg_len), :]

        def block(base, windows):
            windows = list(windows)
            for step in range(turn):
                made = []
                for s in range(2):
                    seen = list(windows[s]) + [row(s, base + step)]
                    made.append(tree_sum([taps[s][i] * seen[-1 - i] for i in range(tap_count)]))
                    windows[s] = tuple(seen[1:])
                driven_ref[tile, base + step] = made[0] * made[1]
            return tuple(windows)

        windows = tuple(tuple(row(s, j - (tap_count - 1)) for j in range(tap_count - 1)) for s in range(2))
        lax.fori_loop(0, seg_len // turn, lambda b, w: block(b * turn, w), windows)
        for j in range(tap_count - 1):
            driven_ref[tile, PAD + j, 0:1, :] = jnp.where(first, driven_ref[tile, PAD + j, 0:1, :], 0.0)

        if tile == 0:
            small[1].wait()
        decays = [jnp.broadcast_to(decay_ref[n : n + 1, lanes], (SEGS, LANES)) for n in range(poles)]

        def scan(b, states):
            states = list(states)
            for step in range(turn):
                value = driven_ref[tile, b * turn + step]
                states = [d * s + value for d, s in zip(decays, states)]
            return tuple(states)

        zero = jnp.zeros((SEGS, LANES), F32)
        ends = lax.fori_loop(0, seg_len // turn, scan, (zero,) * poles)
        for n in range(poles):
            total, factor = ends[n], power(decays[n], seg_len)
            for reach in (1, 2, 4):
                moved = jnp.where(sublane >= reach, pltpu.roll(total, reach, 0), 0.0)
                total = total + factor * moved
                factor = factor * factor
            inner_ref[tile, n] = total
            message_ref[n : n + 1, lanes] = total[SEGS - 1 : SEGS, :]
    small[2].wait()
    small[3].wait()
    carried = power(decay_ref[...], length) * init_ref[0]
    message_ref[0:poles, :] = message_ref[0:poles, :] + jnp.where(first, carried, 0.0)
    for s in range(3):
        message_ref[poles + s * PAD : poles + (s + 1) * PAD, :] = rim_ref[s].astype(F32)[16 - PAD :]
    for copy in copies:
        copy.wait()


def response_kernel(where_ref, query_in_ref, taps_ref, decay_ref, residues_ref, driven_ref, inner_ref, weight_hbm, response_ref, query_ref, mine_ref, wide_ref, weight_sems):
    poles = decay_ref.shape[0]
    tap_count = taps_ref.shape[1]
    lag = tap_count - 1
    length, channels = query_in_ref.shape[2:]
    tiles = channels // LANES
    seg_len, turn = segments(length)
    copies = weight_columns(weight_hbm, mine_ref, where_ref[1], weight_sems)
    for copy in copies:
        copy.start()
    sublane = lax.broadcasted_iota(jnp.int32, (SEGS, LANES), 0)
    for tile in range(tiles):
        lanes = slice(tile * LANES, (tile + 1) * LANES)
        wide_ref[0:EDGE, :] = jnp.zeros((EDGE, LANES), F32)
        wide_ref[EDGE : EDGE + length, :] = query_in_ref[0, 0, :, lanes].astype(F32)
        taps = [jnp.broadcast_to(taps_ref[0, i : i + 1, lanes], (SEGS, LANES)) for i in range(tap_count)]

        def row(j):
            return wide_ref[pl.ds(PAD + j, SEGS, stride=seg_len), :]

        def fir(b, window):
            window = list(window)
            for step in range(turn):
                window.append(row(b * turn + step))
                query_ref[tile, b * turn + step] = tree_sum([taps[i] * window[-1 - i] for i in range(tap_count)])
                window = window[1:]
            return tuple(window)

        lax.fori_loop(0, seg_len // turn, fir, tuple(row(j - lag) for j in range(lag)))

        decays = [jnp.broadcast_to(decay_ref[n : n + 1, lanes], (SEGS, LANES)) for n in range(poles)]
        weights = [jnp.broadcast_to(residues_ref[n : n + 1, lanes], (SEGS, LANES)) for n in range(poles)]
        states = [jnp.where(sublane == 0, 0.0, pltpu.roll(inner_ref[tile, n], 1, 0)) for n in range(poles)]

        def scan(b, states):
            states = list(states)
            for step in range(turn):
                value = driven_ref[tile, b * turn + step]
                states = [d * s + value for d, s in zip(decays, states)]
                response_ref[tile, b * turn + step] = tree_sum([r * s for r, s in zip(weights, states)])
            return tuple(states)

        for b in range(seg_len // turn):
            states = scan(b, states)
    for copy in copies:
        copy.wait()


def gated_kernel(where_ref, message_ref, head_in_ref, taps_ref, decay_ref, residues_ref, init_ref, response_ref, query_ref, gated_ref, head_ref, start_ref, out_ref, early_ref):
    first = where_ref[0] == 0
    poles = decay_ref.shape[0]
    tap_count = taps_ref.shape[1]
    lag = tap_count - 1
    length, channels = gated_ref.shape
    tiles = channels // LANES
    seg_len, turn = segments(length)
    sublane = lax.broadcasted_iota(jnp.int32, (SEGS, LANES), 0)

    heads = []
    for s in range(3):
        head_ref[0:PAD, :] = jnp.where(first, 0.0, message_ref[poles + s * PAD : poles + (s + 1) * PAD, :])
        head_ref[PAD : PAD + 16, :] = head_in_ref[s, 0, 0:16, :].astype(F32)
        heads.append(tree_sum([taps_ref[s, i : i + 1, :] * head_ref[PAD - i : 2 * PAD - i, :] for i in range(tap_count)]))
    head_query = heads[0]
    counted = jnp.where(first, 0.0, heads[1] * heads[2])
    decay, residues = decay_ref[...], residues_ref[...]
    state = jnp.where(first, init_ref[0], message_ref[0:poles, :])
    for j in range(lag):
        state = decay * state + counted[j : j + 1, :]
        early_ref[j : j + 1, :] = jnp.sum(residues * state, axis=0, keepdims=True)
    state = state * residues
    start_ref[0:poles, :] = state / power(decay, PAD + lag)
    start_ref[poles:, :] = state * power(decay, seg_len - PAD - lag)

    for tile in range(tiles):
        lanes = slice(tile * LANES, (tile + 1) * LANES)
        decays = [jnp.broadcast_to(decay_ref[n : n + 1, lanes], (SEGS, LANES)) for n in range(poles)]
        states = []
        for n in range(poles):
            factor = power(decays[n], seg_len)
            spread = jnp.broadcast_to(start_ref[poles + n : poles + n + 1, lanes], (SEGS, LANES))
            before = sublane - 1
            for bit in (1, 2, 4):
                spread = jnp.where(jnp.bitwise_and(before, bit) != 0, spread * factor, spread)
                factor = factor * factor
            own = jnp.broadcast_to(start_ref[n : n + 1, lanes], (SEGS, LANES))
            states.append(jnp.where(sublane == 0, own, spread))

        def block(b, states):
            states = list(states)
            for step in range(turn):
                at = b * turn + step
                states = [d * s for d, s in zip(decays, states)]
                total = response_ref[tile, at] + tree_sum(states)
                out_ref[pl.ds(at, SEGS, stride=seg_len), :] = total * query_ref[tile, at]
            return tuple(states)

        for b in range(seg_len // turn):
            states = block(b, states)
        for j in range(lag):
            total = response_ref[tile, PAD + j, 0:1, :] + early_ref[j : j + 1, lanes]
            out_ref[PAD + j : PAD + j + 1, :] = total * head_query[j : j + 1, lanes]
        gated_ref[:, lanes] = out_ref[PAD : PAD + length, :].astype(BF16)


def relative(index, high, order):
    value = high << (order[0] - 1)
    count = len(order) - 1
    for place, bit in enumerate(order[1:]):
        value = value | (((index >> (count - 1 - place)) & 1) << (bit - 1))
    return value


def sides(part, where_ref, weight_ref, index):
    _, _, column, columns = part.box
    blocks = [relative(index, high, part.order) ^ where_ref[2] for high in (1, 0)]
    return jnp.concatenate([weight_ref[block, :, column : column + columns] for block in blocks], axis=1)


def project_kernel(part, where_ref, own_ref, other_ref, mine_ref, theirs_ref, order_ref, send_ref, keep_ref):
    row, rows, _, columns = part.box
    wide = jnp.concatenate([own_ref[row : row + rows, :], other_ref[row : row + rows, :]], axis=1)

    def step(index):
        both = jnp.concatenate([sides(part, where_ref, ref, index) for ref in (mine_ref, theirs_ref)], axis=0)
        total = jnp.dot(wide, both, preferred_element_type=F32)
        send_ref[index] = total[:, :columns].astype(BF16)
        keep_ref[index] = total[:, columns:]

    for index in range(send_ref.shape[0]):
        step(index)


def project_own_kernel(part, where_ref, own_ref, mine_ref, out_ref):
    row, rows, _, _ = part.box

    def step(index):
        out_ref[index] = jnp.dot(own_ref[row : row + rows, :], sides(part, where_ref, mine_ref, index), preferred_element_type=F32)

    for index in range(out_ref.shape[0]):
        step(index)


def project_other_kernel(part, where_ref, sum_ref, other_ref, theirs_ref, send_ref, keep_ref):
    row, rows, _, columns = part.box

    def step(index):
        total = sum_ref[index] + jnp.dot(other_ref[row : row + rows, :], sides(part, where_ref, theirs_ref, index), preferred_element_type=F32)
        send_ref[index] = total[:, :columns].astype(BF16)
        keep_ref[index] = total[:, columns:]

    for index in range(send_ref.shape[0]):
        step(index)


def merge_kernel(keep_ref, received_ref, order_ref, send_ref, kept_ref):
    half = kept_ref.shape[0]
    send_ref[...] = (keep_ref[half:] + received_ref[half:].astype(F32)).astype(BF16)
    kept_ref[...] = keep_ref[:half] + received_ref[:half].astype(F32)


def finish_kernel(keep_ref, received_ref, order_ref, out_ref):
    out_ref[...] = (keep_ref[0] + received_ref[0].astype(F32)).astype(BF16)


def gather_kernel(boxes, *refs):
    count = len(boxes) - 1
    pieces, (keep_ref, received_ref, order_ref, out_ref, last_ref, sems) = refs[:count], refs[count:]
    copies = []
    for at, (piece, (row, rows, column, columns)) in enumerate(zip(list(pieces) + [last_ref], boxes)):
        if at == count:
            last_ref[...] = (keep_ref[0] + received_ref[0].astype(F32)).astype(BF16)
        place = out_ref.at[0, pl.ds(row, rows), pl.ds(column, columns)]
        copies.append(pltpu.make_async_copy(piece, place, sems.at[at]))
        copies[-1].start()
    for copy in copies:
        copy.wait()


SMEM = pl.BlockSpec(memory_space=pltpu.SMEM)
VMEM = pl.BlockSpec(memory_space=pltpu.VMEM)
HBM = pl.BlockSpec(memory_space=pltpu.HBM)
ANYWHERE = pl.BlockSpec(memory_space=pl.ANY)
LIMIT = 24 * 1024 * 1024
QUICK = pl.CostEstimate(flops=1, bytes_accessed=1, transcendentals=0)


def in_hbm(x):
    return pltpu.with_memory_space_constraint(x, pltpu.MemorySpace.HBM)


@dataclasses.dataclass(frozen=True)
class Part:
    box: tuple
    order: tuple


def project(part, where, own, other, mine, theirs, ordered):
    channels = own.shape[1]
    halves = mine.shape[0]
    rest = halves // 2
    _, rows, _, columns = part.box
    return pl.pallas_call(
        functools.partial(project_kernel, part),
        out_shape=(jax.ShapeDtypeStruct((rest, rows, columns), BF16), jax.ShapeDtypeStruct((rest, rows, columns), F32)),
        in_specs=[SMEM, VMEM, VMEM, VMEM, VMEM, ANYWHERE],
        out_specs=(VMEM, VMEM),
        compiler_params=pltpu.CompilerParams(vmem_limit_bytes=LIMIT),
        cost_estimate=QUICK,
        name="project",
    )(where, own, other, mine, theirs, ordered)


def project_own(part, where, own, mine):
    _, rows, _, columns = part.box
    return pl.pallas_call(
        functools.partial(project_own_kernel, part),
        out_shape=jax.ShapeDtypeStruct((mine.shape[0] // 2, rows, 2 * columns), F32),
        in_specs=[SMEM, VMEM, VMEM],
        out_specs=VMEM,
        compiler_params=pltpu.CompilerParams(vmem_limit_bytes=LIMIT),
        cost_estimate=QUICK,
        name="project_own",
    )(where, own, mine)


def project_other(part, where, total, other, theirs):
    _, rows, _, columns = part.box
    shape = (total.shape[0], rows, columns)
    return pl.pallas_call(
        functools.partial(project_other_kernel, part),
        out_shape=(jax.ShapeDtypeStruct(shape, BF16), jax.ShapeDtypeStruct(shape, F32)),
        in_specs=[SMEM, VMEM, VMEM, VMEM],
        out_specs=(VMEM, VMEM),
        compiler_params=pltpu.CompilerParams(vmem_limit_bytes=LIMIT),
        cost_estimate=QUICK,
        name="project_other",
    )(where, total, other, theirs)


def merge(keep, received, ordered):
    half = keep.shape[0] // 2
    shape = (half,) + keep.shape[1:]
    return pl.pallas_call(
        merge_kernel,
        out_shape=(jax.ShapeDtypeStruct(shape, BF16), jax.ShapeDtypeStruct(shape, F32)),
        in_specs=[VMEM, VMEM, ANYWHERE],
        out_specs=(VMEM, VMEM),
        compiler_params=pltpu.CompilerParams(vmem_limit_bytes=LIMIT),
        cost_estimate=QUICK,
        name="merge",
    )(keep, received, ordered)


def finish(keep, received, ordered):
    return pl.pallas_call(
        finish_kernel,
        out_shape=jax.ShapeDtypeStruct(keep.shape[1:], BF16),
        in_specs=[VMEM, VMEM, ANYWHERE],
        out_specs=VMEM,
        compiler_params=pltpu.CompilerParams(vmem_limit_bytes=LIMIT),
        cost_estimate=QUICK,
        name="finish",
    )(keep, received, ordered)


def gather(pieces, boxes, keep, received, ordered, length, width):
    return pl.pallas_call(
        functools.partial(gather_kernel, boxes),
        out_shape=jax.ShapeDtypeStruct((1, length, width), BF16),
        in_specs=[VMEM] * len(pieces) + [VMEM, VMEM, ANYWHERE],
        out_specs=HBM,
        scratch_shapes=[pltpu.VMEM(keep.shape[1:], BF16), pltpu.SemaphoreType.DMA((len(boxes),))],
        compiler_params=pltpu.CompilerParams(vmem_limit_bytes=LIMIT),
        cost_estimate=QUICK,
        name="gather",
    )(*pieces, keep, received, ordered)


def plan(peers, length, width):
    bits = tuple(range(1, peers.bit_length() - 1))
    far = bits[-2:] + bits[:-2]
    count = width // LANES
    if count == 4 and len(bits) == 3 and length % 48 == 0:
        third = length // 3
        boxes = [(0, length, 0, LANES), (0, length, 2 * LANES, LANES), (0, 2 * third, 3 * LANES, LANES), (2 * third, third, 3 * LANES, LANES), (0, length, LANES, LANES)]
        parts = [Part(box, bits) for box in boxes[:4]] + [Part(boxes[4], far)]
        steps = [(0, -1), (4, -1), (1, -1), (2, -1), (3, -1), (0, 0), (4, 0), (1, 0), (0, 1), (4, 1), (2, 0), (1, 1), (3, 0), (2, 1), (3, 1), (0, 2), (1, 2), (2, 2), (4, 2), (3, 2)]
    else:
        parts = [Part((0, length, LANES * at, LANES), far if at == 1 else bits) for at in range(count)]
        steps = [(at, wave - at - 1) for wave in range(count + len(bits)) for at in range(count) if -1 <= wave - at - 1 < len(bits)]
    return parts, steps


def across(x, bit):
    count = lax.axis_size("tp")
    return lax.ppermute(x, "tp", [(i, i ^ (1 << bit)) for i in range(count)])


def after(x, axis):
    count = lax.axis_size(axis)
    return lax.ppermute(x, axis, [(i, (i + 1) % count) for i in range(count)])


def later_rounds(message, inner_end, streams, taps, decay, init_state):
    first = lax.axis_index("ctx") == 0
    poles = decay.shape[0]
    tap_count = taps.shape[1]
    lag = tap_count - 1
    length = streams.shape[2]
    rims = message[poles:].reshape(3, PAD, -1)
    joined = jnp.concatenate([rims, streams[:, 0, :PAD].astype(F32)], axis=1)
    featured = sum(taps[:, i][:, None, :] * joined[:, PAD - i : 2 * PAD - i, :] for i in range(tap_count))
    head = jnp.where(first, 0.0, featured[1] * featured[2])
    local = jnp.where(first, 0.0, inner_end)

    def one(_, incoming):
        state = jnp.where(first, init_state[0], incoming)
        for j in range(lag):
            state = decay * state + head[j][None]
        ended = jnp.where(first, inner_end, local + power(decay, length - lag) * state)
        return after(ended, "ctx")

    state = lax.fori_loop(0, lax.axis_size("ctx") - 2, one, message[:poles])
    return jnp.concatenate([state, message[poles:]], axis=0)


def per_device(streams, taps, decay, residues, init_state, out_weight):
    length, channels = streams.shape[2:]
    poles = decay.shape[0]
    tiles = channels // LANES
    seg_len, turn = segments(length)
    peers = lax.axis_size("tp")
    width = out_weight.shape[1] // peers
    me = lax.axis_index("tp")
    where = jnp.stack([lax.axis_index("ctx"), me & 1, me >> 1]).astype(jnp.int32)
    rows = poles + 3 * PAD
    streams_hbm, weight_hbm = in_hbm(streams), in_hbm(out_weight)
    split = (tiles, seg_len, SEGS, LANES)
    columns = jax.ShapeDtypeStruct((peers // 2, channels, width), BF16)
    driven, inner, message, sent = pl.pallas_call(
        driven_kernel,
        out_shape=(
            jax.ShapeDtypeStruct(split, F32),
            jax.ShapeDtypeStruct((tiles, poles, SEGS, LANES), F32),
            jax.ShapeDtypeStruct((rows, channels), F32),
            columns,
        ),
        in_specs=[SMEM, HBM, HBM, HBM, HBM, HBM],
        out_specs=(VMEM, VMEM, VMEM, VMEM),
        scratch_shapes=[
            pltpu.VMEM((2, EDGE + length + SPARE, LANES), F32),
            pltpu.VMEM((tiles, 2, length, LANES), BF16),
            pltpu.VMEM((3, 16, channels), BF16),
            pltpu.VMEM(taps.shape, F32),
            pltpu.VMEM(decay.shape, F32),
            pltpu.VMEM(init_state.shape, F32),
            pltpu.SemaphoreType.DMA((peers // 2,)),
            pltpu.SemaphoreType.DMA((4 + tiles,)),
        ],
        compiler_params=pltpu.CompilerParams(vmem_limit_bytes=LIMIT),
        cost_estimate=QUICK,
        name="driven",
    )(where, streams_hbm, in_hbm(taps), in_hbm(decay), in_hbm(init_state), weight_hbm)
    passed = after(message, "ctx")
    theirs = across(sent, 0)
    response, query, mine = pl.pallas_call(
        response_kernel,
        out_shape=(
            jax.ShapeDtypeStruct(split, F32),
            jax.ShapeDtypeStruct(split, F32),
            columns,
        ),
        in_specs=[SMEM] + [VMEM] * 6 + [HBM],
        out_specs=(VMEM, VMEM, VMEM),
        scratch_shapes=[pltpu.VMEM((EDGE + length + SPARE, LANES), F32), pltpu.SemaphoreType.DMA((peers // 2,))],
        compiler_params=pltpu.CompilerParams(vmem_limit_bytes=LIMIT),
        cost_estimate=QUICK,
        name="response",
    )(where, streams, taps, decay, residues, driven, inner, weight_hbm)
    if lax.axis_size("ctx") > 2:
        passed = later_rounds(passed, message[:poles], streams, taps, decay, init_state)
    gated = pl.pallas_call(
        gated_kernel,
        out_shape=jax.ShapeDtypeStruct((length, channels), BF16),
        in_specs=[SMEM] + [VMEM] * 8,
        out_specs=VMEM,
        scratch_shapes=[
            pltpu.VMEM((PAD + 16, channels), F32),
            pltpu.VMEM((2 * poles, channels), F32),
            pltpu.VMEM((PAD + length + SPARE, LANES), F32),
            pltpu.VMEM((PAD, channels), F32),
        ],
        compiler_params=pltpu.CompilerParams(vmem_limit_bytes=LIMIT),
        cost_estimate=QUICK,
        name="gated",
    )(where, passed, streams, taps, decay, residues, init_state, response, query)
    other = across(gated, 0)

    parts, steps = plan(peers, length, width)
    flying, kept, finished, ordered = {}, {}, {}, gated
    started = project_own(parts[steps[0][0]], where, gated, mine)
    for at, stage in steps:
        part = parts[at]
        if stage < 0:
            if at == steps[0][0]:
                send, kept[at] = project_other(part, where, started, other, theirs)
            else:
                send, kept[at] = project(part, where, gated, other, mine, theirs, ordered)
            ordered = send
        elif stage + 1 < len(part.order):
            send, kept[at] = merge(kept[at], flying[at], ordered)
            ordered = send
        elif len(finished) + 1 < len(parts):
            ordered = finished[at] = finish(kept[at], flying[at], ordered)
            continue
        else:
            boxes = [parts[done].box for done in finished] + [part.box]
            return gather(list(finished.values()), boxes, kept[at], flying[at], ordered, length, width)
        flying[at] = across(send, part.order[stage + 1])


def solution(mesh):
    in_specs = (
        P(None, None, "ctx", "tp"),
        P(None, None, "tp"),
        P(None, "tp"),
        P(None, "tp"),
        P(None, None, "tp"),
        P("tp", None),
    )
    out_specs = P(None, "ctx", "tp")
    return jax.shard_map(
        per_device, mesh=mesh, in_specs=in_specs, out_specs=out_specs, check_vma=False
    )
```

```python
import dataclasses
import functools

import jax
import jax.numpy as jnp
from jax import lax
from jax.experimental import pallas as pl
from jax.experimental.pallas import tpu as pltpu
from jax.sharding import PartitionSpec as P

F32 = jnp.float32
BF16 = jnp.bfloat16
LANES = 128
SEGS = 8
PAD = 8
EDGE = 2 * PAD
SPARE = 64


def power(base, exponent):
    result, square = None, base
    while exponent:
        if exponent & 1:
            result = square if result is None else result * square
        exponent >>= 1
        if exponent:
            square = square * square
    return result


def segments(length):
    seg_len = (length + PAD) // SEGS
    return seg_len, next(n for n in (7, 8, 6, 5, 4, 3, 2, 1) if seg_len % n == 0)


def tree_sum(terms):
    while len(terms) > 1:
        paired = [a + b for a, b in zip(terms[::2], terms[1::2])]
        terms = paired + terms[len(paired) * 2 :]
    return terms[0]


def weight_columns(weight_hbm, ref, side, sems):
    parts, _, width = ref.shape
    copies = []
    for part in range(parts):
        column = pl.multiple_of((2 * part + side) * width, LANES)
        copies.append(pltpu.make_async_copy(weight_hbm.at[:, pl.ds(column, width)], ref.at[part], sems.at[part]))
    return copies


def driven_kernel(where_ref, streams_hbm, taps_hbm, decay_hbm, init_hbm, weight_hbm, driven_ref, inner_ref, message_ref, sent_ref, wide_ref, streams_ref, rim_ref, taps_ref, decay_ref, init_ref, weight_sems, sems):
    first = where_ref[0] == 0
    core = where_ref[1]
    poles = decay_ref.shape[0]
    tap_count = taps_ref.shape[1]
    length, channels = streams_hbm.shape[2:]
    tiles = channels // LANES
    seg_len, turn = segments(length)
    small = [
        pltpu.make_async_copy(taps_hbm, taps_ref, sems.at[0]),
        pltpu.make_async_copy(decay_hbm, decay_ref, sems.at[1]),
        pltpu.make_async_copy(init_hbm, init_ref, sems.at[2]),
        pltpu.make_async_copy(streams_hbm.at[:, 0, length - 16 :], rim_ref, sems.at[3]),
    ]
    loads = []
    for tile in range(tiles):
        lanes = pl.ds(tile * LANES, LANES)
        loads.append(pltpu.make_async_copy(streams_hbm.at[1:3, 0, :, lanes], streams_ref.at[tile], sems.at[4 + tile]))
    loads[0].start()
    for copy in small[:2] + loads[1:] + small[2:]:
        copy.start()
    copies = weight_columns(weight_hbm, sent_ref, 1 - core, weight_sems)
    small[0].wait()
    sublane = lax.broadcasted_iota(jnp.int32, (SEGS, LANES), 0)
    for tile in range(tiles):
        lanes = slice(tile * LANES, (tile + 1) * LANES)
        loads[tile].wait()
        if tile < 2:
            for copy in copies[tile::2]:
                copy.start()
        for s in range(2):
            wide_ref[s, 0:EDGE, :] = jnp.zeros((EDGE, LANES), F32)
            wide_ref[s, EDGE : EDGE + length, :] = streams_ref[tile, s].astype(F32)
        taps = [[jnp.broadcast_to(taps_ref[1 + s, i : i + 1, lanes], (SEGS, LANES)) for i in range(tap_count)] for s in range(2)]

        def row(s, j):
            return wide_ref[s, pl.ds(PAD + j, SEGS, stride=seg_len), :]

        def block(base, windows):
            windows = list(windows)
            for step in range(turn):
                made = []
                for s in range(2):
                    seen = list(windows[s]) + [row(s, base + step)]
                    made.append(tree_sum([taps[s][i] * seen[-1 - i] for i in range(tap_count)]))
                    windows[s] = tuple(seen[1:])
                driven_ref[tile, base + step] = made[0] * made[1]
            return tuple(windows)

        windows = tuple(tuple(row(s, j - (tap_count - 1)) for j in range(tap_count - 1)) for s in range(2))
        lax.fori_loop(0, seg_len // turn, lambda b, w: block(b * turn, w), windows)
        for j in range(tap_count - 1):
            driven_ref[tile, PAD + j, 0:1, :] = jnp.where(first, driven_ref[tile, PAD + j, 0:1, :], 0.0)

        if tile == 0:
            small[1].wait()
        decays = [jnp.broadcast_to(decay_ref[n : n + 1, lanes], (SEGS, LANES)) for n in range(poles)]

        def scan(b, states):
            states = list(states)
            for step in range(turn):
                value = driven_ref[tile, b * turn + step]
                states = [d * s + value for d, s in zip(decays, states)]
            return tuple(states)

        zero = jnp.zeros((SEGS, LANES), F32)
        ends = lax.fori_loop(0, seg_len // turn, scan, (zero,) * poles)
        for n in range(poles):
            total, factor = ends[n], power(decays[n], seg_len)
            for reach in (1, 2, 4):
                moved = jnp.where(sublane >= reach, pltpu.roll(total, reach, 0), 0.0)
                total = total + factor * moved
                factor = factor * factor
            inner_ref[tile, n] = total
            message_ref[n : n + 1, lanes] = total[SEGS - 1 : SEGS, :]
    small[2].wait()
    small[3].wait()
    carried = power(decay_ref[...], length) * init_ref[0]
    message_ref[0:poles, :] = message_ref[0:poles, :] + jnp.where(first, carried, 0.0)
    for s in range(3):
        message_ref[poles + s * PAD : poles + (s + 1) * PAD, :] = rim_ref[s].astype(F32)[16 - PAD :]
    for copy in copies:
        copy.wait()


def response_kernel(where_ref, query_in_ref, taps_ref, decay_ref, residues_ref, driven_ref, inner_ref, weight_hbm, response_ref, query_ref, mine_ref, wide_ref, weight_sems):
    poles = decay_ref.shape[0]
    tap_count = taps_ref.shape[1]
    lag = tap_count - 1
    length, channels = query_in_ref.shape[2:]
    tiles = channels // LANES
    seg_len, turn = segments(length)
    copies = weight_columns(weight_hbm, mine_ref, where_ref[1], weight_sems)
    for copy in copies:
        copy.start()
    sublane = lax.broadcasted_iota(jnp.int32, (SEGS, LANES), 0)
    for tile in range(tiles):
        lanes = slice(tile * LANES, (tile + 1) * LANES)
        wide_ref[0:EDGE, :] = jnp.zeros((EDGE, LANES), F32)
        wide_ref[EDGE : EDGE + length, :] = query_in_ref[0, 0, :, lanes].astype(F32)
        taps = [jnp.broadcast_to(taps_ref[0, i : i + 1, lanes], (SEGS, LANES)) for i in range(tap_count)]

        def row(j):
            return wide_ref[pl.ds(PAD + j, SEGS, stride=seg_len), :]

        def fir(b, window):
            window = list(window)
            for step in range(turn):
                window.append(row(b * turn + step))
                query_ref[tile, b * turn + step] = tree_sum([taps[i] * window[-1 - i] for i in range(tap_count)])
                window = window[1:]
            return tuple(window)

        lax.fori_loop(0, seg_len // turn, fir, tuple(row(j - lag) for j in range(lag)))

        decays = [jnp.broadcast_to(decay_ref[n : n + 1, lanes], (SEGS, LANES)) for n in range(poles)]
        weights = [jnp.broadcast_to(residues_ref[n : n + 1, lanes], (SEGS, LANES)) for n in range(poles)]
        states = [jnp.where(sublane == 0, 0.0, pltpu.roll(inner_ref[tile, n], 1, 0)) for n in range(poles)]

        def scan(b, states):
            states = list(states)
            for step in range(turn):
                value = driven_ref[tile, b * turn + step]
                states = [d * s + value for d, s in zip(decays, states)]
                response_ref[tile, b * turn + step] = tree_sum([r * s for r, s in zip(weights, states)])
            return tuple(states)

        for b in range(seg_len // turn):
            states = scan(b, states)
    for copy in copies:
        copy.wait()


def gated_kernel(where_ref, message_ref, head_in_ref, taps_ref, decay_ref, residues_ref, init_ref, response_ref, query_ref, gated_ref, head_ref, start_ref, out_ref, early_ref):
    first = where_ref[0] == 0
    poles = decay_ref.shape[0]
    tap_count = taps_ref.shape[1]
    lag = tap_count - 1
    length, channels = gated_ref.shape
    tiles = channels // LANES
    seg_len, turn = segments(length)
    sublane = lax.broadcasted_iota(jnp.int32, (SEGS, LANES), 0)

    heads = []
    for s in range(3):
        head_ref[0:PAD, :] = jnp.where(first, 0.0, message_ref[poles + s * PAD : poles + (s + 1) * PAD, :])
        head_ref[PAD : PAD + 16, :] = head_in_ref[s, 0, 0:16, :].astype(F32)
        heads.append(tree_sum([taps_ref[s, i : i + 1, :] * head_ref[PAD - i : 2 * PAD - i, :] for i in range(tap_count)]))
    head_query = heads[0]
    counted = jnp.where(first, 0.0, heads[1] * heads[2])
    decay, residues = decay_ref[...], residues_ref[...]
    state = jnp.where(first, init_ref[0], message_ref[0:poles, :])
    for j in range(lag):
        state = decay * state + counted[j : j + 1, :]
        early_ref[j : j + 1, :] = jnp.sum(residues * state, axis=0, keepdims=True)
    state = state * residues
    start_ref[0:poles, :] = state / power(decay, PAD + lag)
    start_ref[poles:, :] = state * power(decay, seg_len - PAD - lag)

    for tile in range(tiles):
        lanes = slice(tile * LANES, (tile + 1) * LANES)
        decays = [jnp.broadcast_to(decay_ref[n : n + 1, lanes], (SEGS, LANES)) for n in range(poles)]
        states = []
        for n in range(poles):
            factor = power(decays[n], seg_len)
            spread = jnp.broadcast_to(start_ref[poles + n : poles + n + 1, lanes], (SEGS, LANES))
            before = sublane - 1
            for bit in (1, 2, 4):
                spread = jnp.where(jnp.bitwise_and(before, bit) != 0, spread * factor, spread)
                factor = factor * factor
            own = jnp.broadcast_to(start_ref[n : n + 1, lanes], (SEGS, LANES))
            states.append(jnp.where(sublane == 0, own, spread))

        def block(b, states):
            states = list(states)
            for step in range(turn):
                at = b * turn + step
                states = [d * s for d, s in zip(decays, states)]
                total = response_ref[tile, at] + tree_sum(states)
                out_ref[pl.ds(at, SEGS, stride=seg_len), :] = total * query_ref[tile, at]
            return tuple(states)

        for b in range(seg_len // turn):
            states = block(b, states)
        for j in range(lag):
            total = response_ref[tile, PAD + j, 0:1, :] + early_ref[j : j + 1, lanes]
            out_ref[PAD + j : PAD + j + 1, :] = total * head_query[j : j + 1, lanes]
        gated_ref[:, lanes] = out_ref[PAD : PAD + length, :].astype(BF16)


def relative(index, high, order):
    value = high << (order[0] - 1)
    count = len(order) - 1
    for place, bit in enumerate(order[1:]):
        value = value | (((index >> (count - 1 - place)) & 1) << (bit - 1))
    return value


def sides(part, where_ref, weight_ref, index):
    _, _, column, columns = part.box
    blocks = [relative(index, high, part.order) ^ where_ref[2] for high in (1, 0)]
    return jnp.concatenate([weight_ref[block, :, column : column + columns] for block in blocks], axis=1)


def project_kernel(part, where_ref, own_ref, other_ref, mine_ref, theirs_ref, order_ref, send_ref, keep_ref):
    row, rows, _, columns = part.box
    wide = jnp.concatenate([own_ref[row : row + rows, :], other_ref[row : row + rows, :]], axis=1)

    def step(index):
        both = jnp.concatenate([sides(part, where_ref, ref, index) for ref in (mine_ref, theirs_ref)], axis=0)
        total = jnp.dot(wide, both, preferred_element_type=F32)
        send_ref[index] = total[:, :columns].astype(BF16)
        keep_ref[index] = total[:, columns:]

    for index in range(send_ref.shape[0]):
        step(index)


def project_own_kernel(part, where_ref, own_ref, mine_ref, out_ref):
    row, rows, _, _ = part.box
    count, _, wide = out_ref.shape
    blocks = jnp.concatenate([sides(part, where_ref, mine_ref, index) for index in range(count)], axis=1)
    total = jnp.dot(own_ref[row : row + rows, :], blocks, preferred_element_type=F32)
    for index in range(count):
        out_ref[index] = total[:, index * wide : (index + 1) * wide]


def project_other_kernel(part, where_ref, sum_ref, other_ref, theirs_ref, send_ref, keep_ref):
    row, rows, _, columns = part.box
    count, _, wide = sum_ref.shape
    blocks = jnp.concatenate([sides(part, where_ref, theirs_ref, index) for index in range(count)], axis=1)
    product = jnp.dot(other_ref[row : row + rows, :], blocks, preferred_element_type=F32)
    for index in range(count):
        total = sum_ref[index] + product[:, index * wide : (index + 1) * wide]
        send_ref[index] = total[:, :columns].astype(BF16)
        keep_ref[index] = total[:, columns:]


def merge_kernel(keep_ref, received_ref, order_ref, send_ref, kept_ref):
    half = kept_ref.shape[0]
    send_ref[...] = (keep_ref[half:] + received_ref[half:].astype(F32)).astype(BF16)
    kept_ref[...] = keep_ref[:half] + received_ref[:half].astype(F32)


def finish_kernel(keep_ref, received_ref, order_ref, out_ref):
    out_ref[...] = (keep_ref[0] + received_ref[0].astype(F32)).astype(BF16)


def gather_kernel(boxes, *refs):
    count = len(boxes) - 1
    pieces, (keep_ref, received_ref, order_ref, out_ref, last_ref, sems) = refs[:count], refs[count:]
    copies = []
    for at, (piece, (row, rows, column, columns)) in enumerate(zip(list(pieces) + [last_ref], boxes)):
        if at == count:
            last_ref[...] = (keep_ref[0] + received_ref[0].astype(F32)).astype(BF16)
        place = out_ref.at[0, pl.ds(row, rows), pl.ds(column, columns)]
        copies.append(pltpu.make_async_copy(piece, place, sems.at[at]))
        copies[-1].start()
    for copy in copies:
        copy.wait()


SMEM = pl.BlockSpec(memory_space=pltpu.SMEM)
VMEM = pl.BlockSpec(memory_space=pltpu.VMEM)
HBM = pl.BlockSpec(memory_space=pltpu.HBM)
ANYWHERE = pl.BlockSpec(memory_space=pl.ANY)
LIMIT = 24 * 1024 * 1024
QUICK = pl.CostEstimate(flops=1, bytes_accessed=1, transcendentals=0)


def in_hbm(x):
    return pltpu.with_memory_space_constraint(x, pltpu.MemorySpace.HBM)


@dataclasses.dataclass(frozen=True)
class Part:
    box: tuple
    order: tuple


def project(part, where, own, other, mine, theirs, ordered):
    channels = own.shape[1]
    halves = mine.shape[0]
    rest = halves // 2
    _, rows, _, columns = part.box
    return pl.pallas_call(
        functools.partial(project_kernel, part),
        out_shape=(jax.ShapeDtypeStruct((rest, rows, columns), BF16), jax.ShapeDtypeStruct((rest, rows, columns), F32)),
        in_specs=[SMEM, VMEM, VMEM, VMEM, VMEM, ANYWHERE],
        out_specs=(VMEM, VMEM),
        compiler_params=pltpu.CompilerParams(vmem_limit_bytes=LIMIT),
        cost_estimate=QUICK,
        name="project",
    )(where, own, other, mine, theirs, ordered)


def project_own(part, where, own, mine):
    _, rows, _, columns = part.box
    return pl.pallas_call(
        functools.partial(project_own_kernel, part),
        out_shape=jax.ShapeDtypeStruct((mine.shape[0] // 2, rows, 2 * columns), F32),
        in_specs=[SMEM, VMEM, VMEM],
        out_specs=VMEM,
        compiler_params=pltpu.CompilerParams(vmem_limit_bytes=LIMIT),
        cost_estimate=QUICK,
        name="project_own",
    )(where, own, mine)


def project_other(part, where, total, other, theirs):
    _, rows, _, columns = part.box
    shape = (total.shape[0], rows, columns)
    return pl.pallas_call(
        functools.partial(project_other_kernel, part),
        out_shape=(jax.ShapeDtypeStruct(shape, BF16), jax.ShapeDtypeStruct(shape, F32)),
        in_specs=[SMEM, VMEM, VMEM, VMEM],
        out_specs=(VMEM, VMEM),
        compiler_params=pltpu.CompilerParams(vmem_limit_bytes=LIMIT),
        cost_estimate=QUICK,
        name="project_other",
    )(where, total, other, theirs)


def merge(keep, received, ordered):
    half = keep.shape[0] // 2
    shape = (half,) + keep.shape[1:]
    return pl.pallas_call(
        merge_kernel,
        out_shape=(jax.ShapeDtypeStruct(shape, BF16), jax.ShapeDtypeStruct(shape, F32)),
        in_specs=[VMEM, VMEM, ANYWHERE],
        out_specs=(VMEM, VMEM),
        compiler_params=pltpu.CompilerParams(vmem_limit_bytes=LIMIT),
        cost_estimate=QUICK,
        name="merge",
    )(keep, received, ordered)


def finish(keep, received, ordered):
    return pl.pallas_call(
        finish_kernel,
        out_shape=jax.ShapeDtypeStruct(keep.shape[1:], BF16),
        in_specs=[VMEM, VMEM, ANYWHERE],
        out_specs=VMEM,
        compiler_params=pltpu.CompilerParams(vmem_limit_bytes=LIMIT),
        cost_estimate=QUICK,
        name="finish",
    )(keep, received, ordered)


def gather(pieces, boxes, keep, received, ordered, length, width):
    return pl.pallas_call(
        functools.partial(gather_kernel, boxes),
        out_shape=jax.ShapeDtypeStruct((1, length, width), BF16),
        in_specs=[VMEM] * len(pieces) + [VMEM, VMEM, ANYWHERE],
        out_specs=HBM,
        scratch_shapes=[pltpu.VMEM(keep.shape[1:], BF16), pltpu.SemaphoreType.DMA((len(boxes),))],
        compiler_params=pltpu.CompilerParams(vmem_limit_bytes=LIMIT),
        cost_estimate=QUICK,
        name="gather",
    )(*pieces, keep, received, ordered)


def plan(peers, length, width):
    bits = tuple(range(1, peers.bit_length() - 1))
    far = bits[-2:] + bits[:-2]
    count = width // LANES
    if count == 4 and len(bits) == 3 and length % 48 == 0:
        third = length // 3
        boxes = [(0, length, 0, LANES), (0, length, 2 * LANES, LANES), (0, 2 * third, 3 * LANES, LANES), (2 * third, third, 3 * LANES, LANES), (0, length, LANES, LANES)]
        parts = [Part(box, bits) for box in boxes[:4]] + [Part(boxes[4], far)]
        steps = [(0, -1), (4, -1), (1, -1), (2, -1), (3, -1), (0, 0), (4, 0), (1, 0), (0, 1), (4, 1), (2, 0), (1, 1), (3, 0), (2, 1), (3, 1), (0, 2), (1, 2), (2, 2), (4, 2), (3, 2)]
    else:
        parts = [Part((0, length, LANES * at, LANES), far if at == 1 else bits) for at in range(count)]
        steps = [(at, wave - at - 1) for wave in range(count + len(bits)) for at in range(count) if -1 <= wave - at - 1 < len(bits)]
    return parts, steps


def across(x, bit):
    count = lax.axis_size("tp")
    return lax.ppermute(x, "tp", [(i, i ^ (1 << bit)) for i in range(count)])


def after(x, axis):
    count = lax.axis_size(axis)
    return lax.ppermute(x, axis, [(i, (i + 1) % count) for i in range(count)])


def later_rounds(message, inner_end, streams, taps, decay, init_state):
    first = lax.axis_index("ctx") == 0
    poles = decay.shape[0]
    tap_count = taps.shape[1]
    lag = tap_count - 1
    length = streams.shape[2]
    rims = message[poles:].reshape(3, PAD, -1)
    joined = jnp.concatenate([rims, streams[:, 0, :PAD].astype(F32)], axis=1)
    featured = sum(taps[:, i][:, None, :] * joined[:, PAD - i : 2 * PAD - i, :] for i in range(tap_count))
    head = jnp.where(first, 0.0, featured[1] * featured[2])
    local = jnp.where(first, 0.0, inner_end)

    def one(_, incoming):
        state = jnp.where(first, init_state[0], incoming)
        for j in range(lag):
            state = decay * state + head[j][None]
        ended = jnp.where(first, inner_end, local + power(decay, length - lag) * state)
        return after(ended, "ctx")

    state = lax.fori_loop(0, lax.axis_size("ctx") - 2, one, message[:poles])
    return jnp.concatenate([state, message[poles:]], axis=0)


def per_device(streams, taps, decay, residues, init_state, out_weight):
    length, channels = streams.shape[2:]
    poles = decay.shape[0]
    tiles = channels // LANES
    seg_len, turn = segments(length)
    peers = lax.axis_size("tp")
    width = out_weight.shape[1] // peers
    me = lax.axis_index("tp")
    where = jnp.stack([lax.axis_index("ctx"), me & 1, me >> 1]).astype(jnp.int32)
    rows = poles + 3 * PAD
    streams_hbm, weight_hbm = in_hbm(streams), in_hbm(out_weight)
    split = (tiles, seg_len, SEGS, LANES)
    columns = jax.ShapeDtypeStruct((peers // 2, channels, width), BF16)
    driven, inner, message, sent = pl.pallas_call(
        driven_kernel,
        out_shape=(
            jax.ShapeDtypeStruct(split, F32),
            jax.ShapeDtypeStruct((tiles, poles, SEGS, LANES), F32),
            jax.ShapeDtypeStruct((rows, channels), F32),
            columns,
        ),
        in_specs=[SMEM, HBM, HBM, HBM, HBM, HBM],
        out_specs=(VMEM, VMEM, VMEM, VMEM),
        scratch_shapes=[
            pltpu.VMEM((2, EDGE + length + SPARE, LANES), F32),
            pltpu.VMEM((tiles, 2, length, LANES), BF16),
            pltpu.VMEM((3, 16, channels), BF16),
            pltpu.VMEM(taps.shape, F32),
            pltpu.VMEM(decay.shape, F32),
            pltpu.VMEM(init_state.shape, F32),
            pltpu.SemaphoreType.DMA((peers // 2,)),
            pltpu.SemaphoreType.DMA((4 + tiles,)),
        ],
        compiler_params=pltpu.CompilerParams(vmem_limit_bytes=LIMIT),
        cost_estimate=QUICK,
        name="driven",
    )(where, streams_hbm, in_hbm(taps), in_hbm(decay), in_hbm(init_state), weight_hbm)
    passed = after(message, "ctx")
    theirs = across(sent, 0)
    response, query, mine = pl.pallas_call(
        response_kernel,
        out_shape=(
            jax.ShapeDtypeStruct(split, F32),
            jax.ShapeDtypeStruct(split, F32),
            columns,
        ),
        in_specs=[SMEM] + [VMEM] * 6 + [HBM],
        out_specs=(VMEM, VMEM, VMEM),
        scratch_shapes=[pltpu.VMEM((EDGE + length + SPARE, LANES), F32), pltpu.SemaphoreType.DMA((peers // 2,))],
        compiler_params=pltpu.CompilerParams(vmem_limit_bytes=LIMIT),
        cost_estimate=QUICK,
        name="response",
    )(where, streams, taps, decay, residues, driven, inner, weight_hbm)
    if lax.axis_size("ctx") > 2:
        passed = later_rounds(passed, message[:poles], streams, taps, decay, init_state)
    gated = pl.pallas_call(
        gated_kernel,
        out_shape=jax.ShapeDtypeStruct((length, channels), BF16),
        in_specs=[SMEM] + [VMEM] * 8,
        out_specs=VMEM,
        scratch_shapes=[
            pltpu.VMEM((PAD + 16, channels), F32),
            pltpu.VMEM((2 * poles, channels), F32),
            pltpu.VMEM((PAD + length + SPARE, LANES), F32),
            pltpu.VMEM((PAD, channels), F32),
        ],
        compiler_params=pltpu.CompilerParams(vmem_limit_bytes=LIMIT),
        cost_estimate=QUICK,
        name="gated",
    )(where, passed, streams, taps, decay, residues, init_state, response, query)
    other = across(gated, 0)

    parts, steps = plan(peers, length, width)
    flying, kept, finished, ordered = {}, {}, {}, gated
    started = project_own(parts[steps[0][0]], where, gated, mine)
    for at, stage in steps:
        part = parts[at]
        if stage < 0:
            if at == steps[0][0]:
                send, kept[at] = project_other(part, where, started, other, theirs)
            else:
                send, kept[at] = project(part, where, gated, other, mine, theirs, ordered)
            ordered = send
        elif stage + 1 < len(part.order):
            send, kept[at] = merge(kept[at], flying[at], ordered)
            ordered = send
        elif len(finished) + 1 < len(parts):
            ordered = finished[at] = finish(kept[at], flying[at], ordered)
            continue
        else:
            boxes = [parts[done].box for done in finished] + [part.box]
            return gather(list(finished.values()), boxes, kept[at], flying[at], ordered, length, width)
        flying[at] = across(send, part.order[stage + 1])


def solution(mesh):
    in_specs = (
        P(None, None, "ctx", "tp"),
        P(None, None, "tp"),
        P(None, "tp"),
        P(None, "tp"),
        P(None, None, "tp"),
        P("tp", None),
    )
    out_specs = P(None, "ctx", "tp")
    return jax.shard_map(
        per_device, mesh=mesh, in_specs=in_specs, out_specs=out_specs, check_vma=False
    )
```
